128 devices in a mesh: seq: 8 (over y_lo, z), ctx: 16 (over y_hi, x, core).
Axes of the slice: x: 4, y: 4 (y_hi: 2, y_lo: 2; y = y_hi * 2 + y_lo), z: 4, core: 2. Of those that a mesh axis runs over, the one named last changes fastest.
Arguments:
- tokens: bfloat16 [16384, 1152], P(('seq', 'ctx')), may hold values from -6 to 6
- prefix_len: int32 [8], P('seq'), may hold values from 204 to 1024
- query_weight: bfloat16 [1152, 1024], P(('seq', 'ctx')), may hold values from -0.5 to 0.5
- key_weight: bfloat16 [1152, 256], P(('seq', 'ctx')), may hold values from -0.1875 to 0.1875
- value_weight: bfloat16 [1152, 256], P(('seq', 'ctx')), may hold values from -0.1875 to 0.1875
- mixing_weight: bfloat16 [1024, 1152], P(('seq', 'ctx')), may hold values from -0.1875 to 0.1875
- gate_weight: bfloat16 [1152, 6912], P(('seq', 'ctx')), may hold values from -0.1875 to 0.1875
- up_weight: bfloat16 [1152, 6912], P(('seq', 'ctx')), may hold values from -0.1875 to 0.1875
- down_weight: bfloat16 [6912, 1152], P(('seq', 'ctx')), may hold values from -0.078125 to 0.078125
- entry_gain: bfloat16 [1152], P(('seq', 'ctx')), may hold values from 0.5 to 1.5
- mixed_gain: bfloat16 [1152], P(('seq', 'ctx')), may hold values from 0.5 to 1.5
- middle_gain: bfloat16 [1152], P(('seq', 'ctx')), may hold values from 0.5 to 1.5
- closing_gain: bfloat16 [1152], P(('seq', 'ctx')), may hold values from 0.5 to 1.5
- cotangent: bfloat16 [16384, 1152], P(('seq', 'ctx')), may hold values from -6 to 6
Outputs:
- layer_output: bfloat16 [16384, 1152], P(('seq', 'ctx'))
- input_delta: float32 [16384, 1152], P(('seq', 'ctx'))
- query_delta: float32 [1152, 1024], P(('seq', 'ctx'))
- key_delta: float32 [1152, 256], P(('seq', 'ctx'))
- value_delta: float32 [1152, 256], P(('seq', 'ctx'))
- mixing_delta: float32 [1024, 1152], P(('seq', 'ctx'))
- gate_delta: float32 [1152, 6912], P(('seq', 'ctx'))
- up_delta: float32 [1152, 6912], P(('seq', 'ctx'))
- down_delta: float32 [6912, 1152], P(('seq', 'ctx'))
- entry_delta: float32 [1152], P(('seq', 'ctx'))
- mixed_delta: float32 [1152], P(('seq', 'ctx'))
- middle_delta: float32 [1152], P(('seq', 'ctx'))
- closing_delta: float32 [1152], P(('seq', 'ctx'))
The draws below stay inside these ranges and needn't reach their ends.
All inputs are finite; a program needn't handle non-finite values.
Results may differ from the reference program's by a relative error of at most 0.025.
Values may be sent and summed in bfloat16 or wider, within the bound.
No kernel may reach another device: no remote copies, remote signals or barrier semaphores. Data moves between devices by JAX's collectives and lax.ppermute only.
A program may use at most 128 MiB of HBM per device.

```python
import jax
import jax.numpy as jnp
from jax import lax

D = 1152
HQ = 4
HD = 256
FF = 6912
SEQ_LEN = 2048
SEQS = 8
TOKENS = 16384


def with_ends(drawn, rng, least, top_value):
    shape = drawn.shape
    spot = [jax.random.randint(jax.random.fold_in(rng, axis), (), 0, shape[axis]) for axis in range(len(shape))]
    drawn = drawn.at[tuple(spot)].set(least)
    longest = shape.index(max(shape))
    spot[longest] = (spot[longest] + 1) % shape[longest]
    return drawn.at[tuple(spot)].set(top_value)


def shard_levels(stream_key, shape, shards, low, largest):
    def one(position, parts):
        heights = jax.random.uniform(jax.random.fold_in(jax.random.fold_in(stream_key, 6), position), (parts,), jnp.float32, low / len(shards), largest / len(shards))
        return jnp.repeat(jnp.exp(heights), shape[position] // parts).reshape((-1,) + (1,) * (len(shape) - position - 1))

    factor_of = one(*shards[0])
    for cut in shards[1:]:
        factor_of = factor_of * one(*cut)
    return factor_of


def gaussian(rng, dims, scale, limit, shards=(), kind=jnp.bfloat16):
    factor_of = shard_levels(rng, dims, shards, -0.22, 0.18) if shards else 1.0
    array = jax.random.normal(rng, dims, jnp.float32) * scale * factor_of
    return jnp.minimum(jnp.maximum(array, -limit), limit).astype(kind)


def setup_inputs(seed: int = 0) -> dict:
    splits = jax.random.split(jax.random.key(seed), 15)
    tokens = gaussian(splits[0], (TOKENS, D), 1.0, 6.0, ((0, 128),))
    prefix_len = with_ends(jax.random.randint(splits[1], (SEQS,), SEQ_LEN // 10, SEQ_LEN // 2 + 1), jax.random.fold_in(splits[1], 1), SEQ_LEN // 10, (SEQ_LEN // 2 + 1) - 1).astype(jnp.int32)
    query_weight = gaussian(splits[2], (D, HQ * HD), (D // 9) ** -0.5, 0.5, ((0, 128),))
    key_weight = gaussian(splits[3], (D, HD), D ** -0.5, 0.1875, ((0, 128),))
    value_weight = gaussian(splits[4], (D, HD), D ** -0.5, 0.1875, ((0, 128),))
    mixing_weight = gaussian(splits[5], (HQ * HD, D), (HQ * HD) ** -0.5, 0.1875, ((0, 128),))
    gate_weight = gaussian(splits[6], (D, FF), D ** -0.5, 0.1875, ((0, 128),))
    up_weight = gaussian(splits[7], (D, FF), D ** -0.5, 0.1875, ((0, 128),))
    down_weight = gaussian(splits[8], (FF, D), FF ** -0.5, 0.078125, ((0, 128),))
    entry_gain = jnp.clip(1.0 + 0.1 * jax.random.normal(splits[9], (D,), jnp.float32), 0.5, 1.5).astype(jnp.bfloat16)
    mixed_gain = jnp.clip(1.0 + 0.1 * jax.random.normal(splits[10], (D,), jnp.float32), 0.5, 1.5).astype(jnp.bfloat16)
    middle_gain = jnp.clip(1.0 + 0.1 * jax.random.normal(splits[11], (D,), jnp.float32), 0.5, 1.5).astype(jnp.bfloat16)
    closing_gain = jnp.clip(1.0 + 0.1 * jax.random.normal(splits[12], (D,), jnp.float32), 0.5, 1.5).astype(jnp.bfloat16)
    cotangent = gaussian(splits[13], (TOKENS, D), 1.0, 6.0, ((0, 128),))
    return dict(tokens=tokens, prefix_len=prefix_len, query_weight=query_weight, key_weight=key_weight, value_weight=value_weight, mixing_weight=mixing_weight, gate_weight=gate_weight, up_weight=up_weight, down_weight=down_weight, entry_gain=entry_gain, mixed_gain=mixed_gain, middle_gain=middle_gain, closing_gain=closing_gain, cotangent=cotangent)


EPS = 1e-06
CAP = 20.0
QSCALE = 0.0625
THETA = 1000000.0

@jax.custom_vjp
def low(v):
    return lax.optimization_barrier(v.astype(jnp.bfloat16)).astype(jnp.float32)

@jax.custom_vjp
def low_back(v):
    return v

def low_keep(v):
    return (low(v), None)

def low_pass(kept, grad):
    return (grad,)

def back_keep(v):
    return (v, None)

def back_low(kept, grad):
    return (low(grad),)
low.defvjp(low_keep, low_pass)
low_back.defvjp(back_keep, back_low)

def rms_scale(values, gain):
    return values * lax.rsqrt(lax.optimization_barrier(jnp.mean(values * values, axis=-1, keepdims=True)) + EPS) * gain

def rotate(values, angles):
    half = values.shape[-1] // 2
    first = values[..., :half]
    second = values[..., half:]
    cosine = jnp.cos(angles)
    sine = jnp.sin(angles)
    return jnp.concatenate([first * cosine - second * sine, second * cosine + first * sine], axis=-1)

def matmul(left, right):
    return jnp.dot(left, right, precision=lax.Precision.HIGHEST)

def sequence_layer(floats, pair):
    query_w, key_w, value_w, mixing_w, gate_w, up_w, down_w, gain_one, gain_two, gain_three, gain_four = floats
    inputs, prefix = pair
    length = inputs.shape[0]
    head = key_w.shape[1]
    heads = query_w.shape[1] // head
    half = head // 2
    positions = jnp.arange(length, dtype=jnp.float32)
    inverse = 1.0 / THETA ** (jnp.arange(half, dtype=jnp.float32) * (2.0 / head))
    angles = positions[:, None] * inverse[None, :]
    entry_in = low(rms_scale(inputs, gain_one))
    query_raw = matmul(entry_in, query_w)
    key_raw = matmul(entry_in, key_w)
    value_raw = matmul(entry_in, value_w)
    queries = low(rotate(low_back(query_raw).reshape(length, heads, head), angles[:, None, :]) * QSCALE)
    keys = low(rotate(low_back(key_raw), angles))
    values = low(low_back(value_raw))
    scores = low_back(jnp.einsum('qhd,kd->hqk', queries, keys, precision=lax.Precision.HIGHEST))
    capped = CAP * jnp.tanh(scores / CAP)
    index = jnp.arange(length, dtype=jnp.int32)
    allowed = (index[None, :] <= index[:, None]) | (index[None, :] < prefix)
    masked = jnp.where(allowed[None], capped, -1e+30)
    top = lax.optimization_barrier(jnp.max(masked, axis=-1, keepdims=True))
    expo = jnp.exp(masked - top)
    total = lax.optimization_barrier(jnp.sum(expo, axis=-1, keepdims=True))
    probs = low(expo / total)
    mixed = jnp.einsum('hqk,kd->qhd', probs, values, precision=lax.Precision.HIGHEST).reshape(length, heads * head)
    attended = low(low_back(mixed))
    projected = low_back(matmul(attended, mixing_w))
    second = inputs + rms_scale(projected, gain_two)
    middle_in = low(rms_scale(second, gain_three))
    gate = low_back(matmul(middle_in, gate_w))
    up = low_back(matmul(middle_in, up_w))
    hidden = low(jax.nn.gelu(gate, approximate=True) * up)
    feed = low_back(matmul(hidden, down_w))
    return second + rms_scale(feed, gain_four)

def reference(tokens, prefix_len, query_weight, key_weight, value_weight, mixing_weight, gate_weight, up_weight, down_weight, entry_gain, mixed_gain, middle_gain, closing_gain, cotangent):
    width = tokens.shape[1]
    count = prefix_len.shape[0]
    floats = tuple((w.astype(jnp.float32) for w in (query_weight, key_weight, value_weight, mixing_weight, gate_weight, up_weight, down_weight, entry_gain, mixed_gain, middle_gain, closing_gain)))
    inputs = tokens.astype(jnp.float32).reshape(count, -1, width)
    step = jax.checkpoint(sequence_layer)

    def forward(inputs, floats):
        return lax.map(lambda pair: step(floats, pair), (inputs, prefix_len))
    result, pullback = jax.vjp(forward, inputs, floats)
    input_grad, weight_grads = pullback(cotangent.astype(jnp.float32).reshape(count, -1, width))
    query_g, key_g, value_g, mixing_g, gate_g, up_g, down_g, one_g, two_g, three_g, four_g = weight_grads
    return (result.reshape(-1, width).astype(jnp.bfloat16), input_grad.reshape(-1, width), query_g, key_g, value_g, mixing_g, gate_g, up_g, down_g, one_g, two_g, three_g, four_g)
```

```python
import jax
import jax.numpy as jnp
from jax import lax
from jax.sharding import Mesh
from jax.sharding import PartitionSpec as P

EPS = 1e-06
CAP = 20.0
QSCALE = 0.0625
THETA = 1000000.0

AXES = ("yl", "z", "yh", "x", "c")
SIZES = (2, 4, 2, 4, 2)
PLANE = ("z", "yh", "yl")
RING = ("x", "c")


def moved(step):
    pairs = []
    for yl in range(2):
        for z in range(4):
            for yh in range(2):
                for x in range(4):
                    for c in range(2):
                        to = step(yh * 2 + yl, z, x, c)
                        y2, z2, x2, c2 = (to[0] % 4, to[1] % 4, to[2] % 4, to[3] % 2)
                        here = (((yl * 4 + z) * 2 + yh) * 4 + x) * 2 + c
                        there = (((y2 % 2 * 4 + z2) * 2 + y2 // 2) * 4 + x2) * 2 + c2
                        pairs.append((here, there))
    return pairs


HOPS = {
    "c": moved(lambda y, z, x, c: (y, z, x, c + 1)),
    "y2": moved(lambda y, z, x, c: (y + 2, z, x, c)),
}
for n in (1, 2, 3):
    HOPS["x", n] = moved(lambda y, z, x, c: (y, z, x + n, c))
    HOPS["y", n] = moved(lambda y, z, x, c: (y + n, z, x, c))
    HOPS["z", n] = moved(lambda y, z, x, c: (y, z + n, x, c))


def hop(values, way):
    return lax.ppermute(values, AXES, HOPS[way])


def rms_scale(values, gain):
    return values * lax.rsqrt(jnp.mean(values * values, axis=-1, keepdims=True) + EPS) * gain


def rotate(values, angles):
    half = values.shape[-1] // 2
    first = values[..., :half]
    second = values[..., half:]
    cosine = jnp.cos(angles)
    sine = jnp.sin(angles)
    return jnp.concatenate(
        [first * cosine - second * sine, second * cosine + first * sine], axis=-1
    )


def outer(left, right):
    return lax.dot_general(
        left, right, (((0,), (0,)), ((), ())), preferred_element_type=jnp.float32
    )


def through(left, weight):
    return lax.dot_general(
        left, weight, (((1,), (1,)), ((), ())), preferred_element_type=jnp.float32
    )


def product(left, right):
    return jnp.dot(left, right, preferred_element_type=jnp.float32)


def low(values):
    return values.astype(jnp.bfloat16)


def gated(gate, up):
    return jax.nn.gelu(gate, approximate=True) * up


def ring_rows(rows):
    near = jnp.concatenate([rows, hop(rows, ("x", 1)), hop(rows, ("x", 3)), hop(rows, ("x", 2))])
    return near, hop(near, "c")


def ring_sums(near, far):
    count = near.shape[0] // 4
    both = low(near.astype(jnp.float32) + hop(far, "c").astype(jnp.float32))
    own, back, ahead, across = (both[k * count : (k + 1) * count] for k in range(4))
    parts = (hop(back, ("x", 3)), hop(ahead, ("x", 1)), hop(across, ("x", 2)))
    total = own.astype(jnp.float32)
    for part in parts:
        total = total + part.astype(jnp.float32)
    return total


def gather_all(rows):
    for axis in ("z", "y", "x"):
        rows = jnp.concatenate([rows, *(hop(rows, (axis, n)) for n in (3, 2, 1))])
    return jnp.concatenate([rows, hop(rows, "c")])


def scatter_all(term):
    half = term.shape[0] // 2
    term = term[:half].astype(jnp.float32) + hop(term[half:], "c").astype(jnp.float32)
    for axis in ("x", "y", "z"):
        term = low(term)
        cut = term.shape[0] // 4
        parts = [hop(term[n * cut : (n + 1) * cut], (axis, n)) for n in (1, 2, 3)]
        term = term[:cut].astype(jnp.float32)
        for part in parts:
            term = term + part.astype(jnp.float32)
    return term


def by_distance(size):
    here = {axis: lax.axis_index(axis) for axis in AXES}
    block = size // 128
    place = jnp.arange(size, dtype=jnp.int32)
    r, q = (place % block, place // block)
    z = (here["z"] + q) % 4
    y = (here["yh"] * 2 + here["yl"] + q // 4) % 4
    x = (here["x"] + q // 16) % 4
    c = (here["c"] + q // 64) % 2
    source = ((((y % 2 * 4 + z) * 2 + y // 2) * 4 + x) * 2 + c) * block + r
    return low(jnp.arange(size, dtype=jnp.int32)[:, None] == source[None, :])


def body(
    tokens,
    prefix_len,
    query_weight,
    key_weight,
    value_weight,
    mixing_weight,
    gate_weight,
    up_weight,
    down_weight,
    entry_gain,
    mixed_gain,
    middle_gain,
    closing_gain,
    cotangent,
):
    count, width = tokens.shape
    head = key_weight.shape[1]
    heads = query_weight.shape[1] // head
    half = head // 2
    own = gate_weight.shape[0]
    units = down_weight.shape[0]
    units_pad = -(-units // 8) * 8
    hidden_units = 16 * units_pad
    wide = 2 * hidden_units
    own_mix = mixing_weight.shape[0]
    x, c, yh = (lax.axis_index("x"), lax.axis_index("c"), lax.axis_index("yh"))

    def columns(weight):
        cut = weight.reshape(own, 2, 4, 2, 8, units)
        cut = jnp.pad(cut, ((0, 0),) * 5 + ((0, units_pad - units),))
        return cut.transpose(4, 0, 2, 3, 1, 5).reshape(8, own, hidden_units)

    gate_up = jnp.concatenate([columns(gate_weight), columns(up_weight)], axis=2)
    mixing_own = jnp.pad(mixing_weight, ((0, 0), (0, wide - width)))
    mixing_own = jnp.broadcast_to(mixing_own, (8, own_mix, wide))
    ring = lax.all_to_all(
        jnp.concatenate([gate_up, mixing_own], axis=1), RING, 0, 0, tiled=True
    )
    down_own = jnp.pad(down_weight, ((0, units_pad - units), (0, wide - width)))
    plane = lax.all_gather(
        jnp.concatenate(
            [
                ring[:, :own].reshape(8 * own, wide),
                down_own,
                ring[:, own:].reshape(8 * own_mix, wide),
            ]
        ),
        PLANE,
        axis=0,
    )
    ends = (8 * own, 8 * own + units_pad)
    gate_up_full = (
        plane[:, : ends[0]].reshape(4, 2, 2, ends[0], wide).transpose(2, 0, 1, 3, 4)
    ).reshape(width, wide)
    down_full = plane[:, ends[0] : ends[1], :width].reshape(hidden_units, width)
    mixing_full = (
        plane[:, ends[1] :, :width].reshape(4, 2, 2, 8 * own_mix, width).transpose(2, 0, 1, 3, 4)
    ).reshape(heads * head, width)

    qkv_own = jnp.concatenate([query_weight, key_weight, value_weight], axis=1)
    gains_own = jnp.stack([entry_gain, mixed_gain, middle_gain, closing_gain], axis=1)
    gathered = gather_all(
        jnp.concatenate([qkv_own, jnp.pad(gains_own, ((0, 0), (0, 124)))], axis=1)
    )
    qkv_full = gathered[:, : qkv_own.shape[1]]
    entry_order = by_distance(width)
    gains = lax.dot_general(
        gathered[:, qkv_own.shape[1] :],
        entry_order,
        (((0,), (1,)), ((), ())),
        preferred_element_type=jnp.float32,
    )
    entry_scale, mixed_scale, middle_scale, closing_scale = (gains[k] for k in range(4))

    def positions(xs, ys, cs):
        place = ((yh ^ ys) * 4 + (x + xs) % 4) * 2 + (c ^ cs)
        return place * count + jnp.arange(count, dtype=jnp.int32)

    query_pos = positions(0, 0, 0)
    key_pos = jnp.concatenate(
        [positions(xs, ys, cs) for cs in (0, 1) for xs in (0, 3, 1, 2) for ys in (0, 1)]
    )
    length = key_pos.shape[0]
    allowed = (key_pos[None, :] <= query_pos[:, None]) | (key_pos[None, :] < prefix_len[0])
    inverse = 1.0 / THETA ** (jnp.arange(half, dtype=jnp.float32) * (2.0 / head))
    angles = query_pos.astype(jnp.float32)[:, None] * inverse[None, :]
    inputs = tokens.astype(jnp.float32)

    entry_in = low(rms_scale(inputs, entry_scale))
    entry_near = low(product(entry_in, entry_order))
    qkv = product(entry_near, qkv_full)
    query_raw, key_raw, value_raw = jnp.split(qkv, [heads * head, (heads + 1) * head], axis=1)
    queries = low(rotate(query_raw.reshape(count, heads, head), angles[:, None, :]) * QSCALE)
    query_rows = queries.transpose(1, 0, 2).reshape(heads * count, head)
    pairs = jnp.concatenate([low(rotate(key_raw, angles)), low(value_raw)], axis=1)
    near, far = ring_rows(jnp.concatenate([pairs, hop(pairs, "y2")]))
    pairs = jnp.concatenate([near, far])
    all_keys, all_values = (pairs[:, :head], pairs[:, head:])

    def probabilities(top, total):
        scores = through(query_rows, all_keys)
        bent = jnp.tanh(scores / CAP)
        masked = jnp.where(
            allowed[None], (CAP * bent).reshape(heads, count, length), -1e30
        ).reshape(heads * count, length)
        if top is None:
            top = jnp.max(masked, axis=1, keepdims=True)
            expo = jnp.exp(masked - top)
            total = jnp.sum(expo, axis=1, keepdims=True)
        else:
            expo = jnp.exp(masked - top)
        return (expo / total, bent, top, total)

    probs, bent, top, total = probabilities(None, None)
    mixed_rows = product(low(probs), all_values)
    attended = low(
        mixed_rows.reshape(heads, count, head).transpose(1, 0, 2).reshape(count, heads * head)
    )
    projected = product(attended, mixing_full)
    second = inputs + rms_scale(projected, mixed_scale)
    middle_in = low(rms_scale(second, middle_scale))

    middle_parts = ring_rows(middle_in)
    gates, ups, hiddens = ([], [], [])
    for rows in middle_parts:
        both = product(rows, gate_up_full)
        gates.append(both[:, :hidden_units])
        ups.append(both[:, hidden_units:])
        hiddens.append(low(gated(gates[-1], ups[-1])))
    feed = ring_sums(*(low(product(hidden, down_full)) for hidden in hiddens))
    layer_output = low(second + rms_scale(feed, closing_scale))

    incoming = cotangent.astype(jnp.float32)
    unused, closing_back = jax.vjp(rms_scale, feed, closing_scale)
    feed_grad, closing_term = closing_back(incoming)
    feed_parts = ring_rows(low(feed_grad))
    lows = []
    for rows, gate, up in zip(feed_parts, gates, ups):
        unused, gated_back = jax.vjp(gated, gate, up)
        gate_grad, up_grad = gated_back(through(rows, down_full))
        lows.append(jnp.concatenate([low(gate_grad), low(up_grad)], axis=1))
    middle_back = ring_sums(*(low(through(rows, gate_up_full)) for rows in lows))
    gate_up_term = low(outer(jnp.concatenate(middle_parts), jnp.concatenate(lows)))
    down_term = low(outer(jnp.concatenate(hiddens), jnp.concatenate(feed_parts)))
    gate_up_term = gate_up_term.reshape(2, 4, 2, 8 * own, wide).transpose(1, 2, 0, 3, 4)
    down_term = jnp.pad(
        down_term.reshape(16, units_pad, width), ((0, 0), (0, 0), (0, wide - width))
    )
    plane_term = jnp.concatenate([gate_up_term.reshape(16, 8 * own, wide), down_term], axis=1)
    plane_sum = lax.psum_scatter(
        plane_term.reshape(-1, wide), PLANE, scatter_dimension=0, tiled=True
    )
    down_delta = plane_sum[8 * own : 8 * own + units, :width].astype(jnp.float32)
    gate_up_sum = lax.all_to_all(
        plane_sum[: 8 * own].reshape(8, own, wide), RING, 0, 0, tiled=True
    )
    gate_up_sum = gate_up_sum.astype(jnp.float32).reshape(8, own, 2, 4, 2, 2, units_pad)
    gate_up_sum = gate_up_sum[..., :units].transpose(2, 1, 5, 3, 4, 0, 6).reshape(2, own, -1)
    gate_delta, up_delta = (gate_up_sum[0], gate_up_sum[1])

    unused, middle_vjp = jax.vjp(rms_scale, second, middle_scale)
    second_part, middle_term = middle_vjp(middle_back)
    second_delta = incoming + second_part
    unused, mixed_vjp = jax.vjp(rms_scale, projected, mixed_scale)
    projected_grad, mixed_term = mixed_vjp(second_delta)
    projected_low = low(projected_grad)
    attended_low = low(through(projected_low, mixing_full))
    attended_near = low(product(attended, by_distance(heads * head)))
    mixing_term = low(outer(attended_near, projected_low))
    mixing_delta = scatter_all(mixing_term)
    back_rows = (
        attended_low.reshape(count, heads, head).transpose(1, 0, 2).reshape(heads * count, head)
    )
    probs, bent, top, total = probabilities(top, total)
    value_term = outer(low(probs), back_rows)
    prob_back = through(back_rows, all_values)
    weighted = jnp.sum(prob_back * probs, axis=1, keepdims=True)
    capped_back = probs * (prob_back - weighted)
    score_low = low(capped_back * (1.0 - bent * bent))
    query_back = product(score_low, all_keys)
    key_term = outer(score_low, query_rows)
    pair_term = low(jnp.concatenate([key_term, value_term], axis=1))
    pair_sum = ring_sums(pair_term[: length // 2], pair_term[length // 2 :])
    pair_sum = pair_sum[:count] + hop(low(pair_sum[count:]), "y2").astype(jnp.float32)
    query_grad = query_back.reshape(heads, count, head).transpose(1, 0, 2) * QSCALE
    query_low = rotate(query_grad, -angles[:, None, :]).reshape(count, heads * head)
    key_low = rotate(pair_sum[:, :head], -angles)
    qkv_low = low(jnp.concatenate([query_low, key_low, pair_sum[:, head:]], axis=1))
    back_near = through(qkv_low, qkv_full)
    back_high = low(back_near)
    back_rest = low(back_near - back_high.astype(jnp.float32))
    entry_back = through(back_high, entry_order) + through(back_rest, entry_order)
    unused, entry_vjp = jax.vjp(rms_scale, inputs, entry_scale)
    input_part, entry_term = entry_vjp(entry_back)
    input_delta = second_delta + input_part

    qkv_term = outer(entry_near, qkv_low)
    gain_terms = jnp.stack([entry_term, mixed_term, middle_term, closing_term])
    gain_terms = jnp.pad(low(gain_terms), ((0, 124), (0, 0)))
    gain_rows = lax.dot_general(
        entry_order, gain_terms, (((0,), (1,)), ((), ())), preferred_element_type=jnp.float32
    )
    qkv_sum = scatter_all(low(jnp.concatenate([qkv_term, gain_rows], axis=1)))
    cuts = [heads * head, (heads + 1) * head, (heads + 2) * head]
    query_delta, key_delta, value_delta, gain_deltas = jnp.split(qkv_sum, cuts, axis=1)
    entry_delta, mixed_delta, middle_delta, closing_delta = (gain_deltas[:, k] for k in range(4))
    return (
        layer_output,
        input_delta,
        query_delta,
        key_delta,
        value_delta,
        mixing_delta,
        gate_delta,
        up_delta,
        down_delta,
        entry_delta,
        mixed_delta,
        middle_delta,
        closing_delta,
    )


def solution(mesh):
    cut = Mesh(mesh.devices.reshape(SIZES), AXES)
    rows = P(AXES, None)
    flat = P(AXES)
    in_specs = (rows, P(("yl", "z")), *(rows,) * 7, *(flat,) * 4, rows)
    out_specs = (*(rows,) * 9, *(flat,) * 4)
    return jax.shard_map(body, mesh=cut, in_specs=in_specs, out_specs=out_specs, check_vma=False)
```

```python
import jax
import jax.numpy as jnp
from jax import lax
from jax.sharding import Mesh
from jax.sharding import PartitionSpec as P

EPS = 1e-06
CAP = 20.0
QSCALE = 0.0625
THETA = 1000000.0

AXES = ("yl", "z", "yh", "x", "c")
SIZES = (2, 4, 2, 4, 2)
PLANE = ("z", "yh", "yl")
RING = ("x", "c")


def moved(step):
    pairs = []
    for yl in range(2):
        for z in range(4):
            for yh in range(2):
                for x in range(4):
                    for c in range(2):
                        to = step(yh * 2 + yl, z, x, c)
                        y2, z2, x2, c2 = (to[0] % 4, to[1] % 4, to[2] % 4, to[3] % 2)
                        here = (((yl * 4 + z) * 2 + yh) * 4 + x) * 2 + c
                        there = (((y2 % 2 * 4 + z2) * 2 + y2 // 2) * 4 + x2) * 2 + c2
                        pairs.append((here, there))
    return pairs


HOPS = {
    "c": moved(lambda y, z, x, c: (y, z, x, c + 1)),
    "y2": moved(lambda y, z, x, c: (y + 2, z, x, c)),
}
for n in (1, 2, 3):
    HOPS["x", n] = moved(lambda y, z, x, c: (y, z, x + n, c))
    HOPS["y", n] = moved(lambda y, z, x, c: (y + n, z, x, c))
    HOPS["z", n] = moved(lambda y, z, x, c: (y, z + n, x, c))


def hop(values, way):
    return lax.ppermute(values, AXES, HOPS[way])


def rms_scale(values, gain):
    return values * lax.rsqrt(jnp.mean(values * values, axis=-1, keepdims=True) + EPS) * gain


def rotate(values, cosine, sine):
    half = values.shape[-1] // 2
    first = values[..., :half]
    second = values[..., half:]
    return jnp.concatenate(
        [first * cosine - second * sine, second * cosine + first * sine], axis=-1
    )


def outer(left, right):
    return lax.dot_general(
        left, right, (((0,), (0,)), ((), ())), preferred_element_type=jnp.float32
    )


def through(left, weight):
    return lax.dot_general(
        left, weight, (((1,), (1,)), ((), ())), preferred_element_type=jnp.float32
    )


def product(left, right):
    return jnp.dot(left, right, preferred_element_type=jnp.float32)


def low(values):
    return values.astype(jnp.bfloat16)


def gated(gate, up):
    return jax.nn.gelu(gate, approximate=True) * up


def ring_rows(rows):
    near = jnp.concatenate([rows, hop(rows, ("x", 1)), hop(rows, ("x", 3)), hop(rows, ("x", 2))])
    return near, hop(near, "c")


def ring_sums(near, far):
    count = near.shape[0] // 4
    both = low(near.astype(jnp.float32) + hop(far, "c").astype(jnp.float32))
    own, back, ahead, across = (both[k * count : (k + 1) * count] for k in range(4))
    parts = (hop(back, ("x", 3)), hop(ahead, ("x", 1)), hop(across, ("x", 2)))
    total = own.astype(jnp.float32)
    for part in parts:
        total = total + part.astype(jnp.float32)
    return total


def stacked(parts):
    cut = parts[0].shape[0]
    rows = cut * len(parts)
    return sum(
        jnp.pad(part, ((n * cut, rows - (n + 1) * cut), (0, 0))) for n, part in enumerate(parts)
    )


def sent(*pairs):
    return lax.optimization_barrier([hop(value, way) for value, way in pairs])


def along(axis, terms):
    return [(terms[n], (axis, n)) for n in (1, 2, 3)]


def added(own, parts):
    total = own.astype(jnp.float32)
    for part in parts:
        total = total + part.astype(jnp.float32)
    return total


def quarters(values):
    cut = values.shape[0] // 4
    return [values[n * cut : (n + 1) * cut] for n in range(4)]


def once(value, *others):
    return lax.optimization_barrier((value, *others))[0]


def one_hot(rows, source, turned=False):
    place = jnp.arange(rows, dtype=jnp.int32)
    if turned:
        return low(source[:, None] == place[None, :])
    return low(place[:, None] == source[None, :])


def by_distance(size):
    here = {axis: lax.axis_index(axis) for axis in AXES}
    block = size // 128
    place = jnp.arange(size, dtype=jnp.int32)
    r, q = (place % block, place // block)
    c, z, y, x = (q, q // 2, q // 8, q // 32)
    z = (here["z"] + z) % 4
    y = (here["yh"] * 2 + here["yl"] + y) % 4
    x = (here["x"] + x) % 4
    c = (here["c"] + c) % 2
    return ((((y % 2 * 4 + z) * 2 + y // 2) * 4 + x) * 2 + c) * block + r


def by_ring(size, core_first):
    block = size // 128
    place = jnp.arange(size, dtype=jnp.int32)
    r, q = (place % block, place // block)
    if core_first:
        c, x, plane = (q // 64, q // 16, q % 16)
    else:
        c, x, plane = (q, q // 32, q // 2 % 16)
    x = (lax.axis_index("x") + x) % 4
    c = (lax.axis_index("c") + c) % 2
    return ((plane * 4 + x) * 2 + c) * block + r


def body(
    tokens,
    prefix_len,
    query_weight,
    key_weight,
    value_weight,
    mixing_weight,
    gate_weight,
    up_weight,
    down_weight,
    entry_gain,
    mixed_gain,
    middle_gain,
    closing_gain,
    cotangent,
):
    count, width = tokens.shape
    head = key_weight.shape[1]
    heads = query_weight.shape[1] // head
    half = head // 2
    own = gate_weight.shape[0]
    units = down_weight.shape[0]
    units_pad = -(-units // 8) * 8
    hidden_units = 16 * units_pad
    wide = 2 * hidden_units
    own_mix = mixing_weight.shape[0]
    x, c, yh = (lax.axis_index("x"), lax.axis_index("c"), lax.axis_index("yh"))

    def columns(weight):
        cut = weight.reshape(own, 2, 4, 2, 8, units)
        cut = jnp.pad(cut, ((0, 0),) * 5 + ((0, units_pad - units),))
        return cut.transpose(4, 0, 2, 3, 1, 5).reshape(4, 2, own, hidden_units)

    def at(values, index, axis):
        return lax.dynamic_index_in_dim(values, index, axis, keepdims=False)

    mine = heads * head // 2

    def share(core):
        queries = query_weight[:, core * mine : (core + 1) * mine]
        return jnp.concatenate([queries, (key_weight, value_weight)[core]], axis=1)

    def picked(first, second):
        return jnp.where(c == 0, first, second)

    gains_own = jnp.stack([entry_gain, mixed_gain, middle_gain, closing_gain], axis=1)
    gains_own = jnp.pad(gains_own, ((0, 0), (0, 124)))
    kept = jnp.concatenate([picked(share(0), share(1)), gains_own], axis=1)
    given = jnp.concatenate([picked(share(1), share(0)), gains_own], axis=1)
    gate_up = jnp.concatenate([columns(gate_weight), columns(up_weight)], axis=3)
    mixing_own = jnp.pad(mixing_weight, ((0, 0), (0, wide - width)))

    blocks, swapped = sent(
        (given, "c"),
        (jnp.concatenate([at(gate_up, 1 - c, 1).reshape(4 * own, wide), mixing_own]), "c"),
    )
    pair_up = jnp.concatenate(
        [at(gate_up, c, 1), swapped[: 4 * own].reshape(4, own, wide)], axis=1
    )
    pair_mixing = jnp.concatenate([mixing_own, swapped[4 * own :]])
    ring = [jnp.concatenate([at(pair_up, (x + n) % 4, 0), pair_mixing]) for n in range(4)]
    blocks = jnp.concatenate([kept, blocks])
    *parts, across = sent(
        *along("x", ring), *((blocks, ("z", n)) for n in (3, 2, 1)), (tokens, "y2")
    )
    ring = jnp.concatenate([ring[0], *parts[:3]])
    blocks = stacked([blocks, *parts[3:]])
    near = jnp.concatenate([tokens, across])
    parts = sent(
        *((near, ("x", n)) for n in (1, 3, 2)), *((blocks, ("y", n)) for n in (3, 2, 1))
    )
    near = jnp.concatenate([near, *parts[:3]])
    blocks = stacked([blocks, *parts[3:]])
    far = hop(near, "c")
    chunks = [blocks, *(hop(blocks, ("x", n)) for n in (3, 2, 1))]
    ring_order = one_hot(width, by_ring(width, False))
    chunks, near_ring, far_ring = lax.optimization_barrier(
        (chunks, low(product(near, ring_order)), low(product(far, ring_order)))
    )
    step = 2 * (own + own_mix)
    place = jnp.arange(4 * step, dtype=jnp.int32)
    q, r = (place // own, place % own)
    up_source = (x - q // 2) % 4 * step + (q % 2 ^ c) * own + r
    q, r = ((place - 8 * own) // own_mix, (place - 8 * own) % own_mix)
    mixing_source = (x - q // 2) % 4 * step + 2 * own + (q % 2 ^ c) * own_mix + r
    source = jnp.where(place < 8 * own, up_source, mixing_source)
    ring = low(outer(one_hot(4 * step, source), ring))
    end = 8 * own
    rest = wide - width
    mixing_half = ring[end:, : width // 2]
    mixing_half = jnp.where(c == 0, mixing_half, ring[end:, width // 2 : width])
    down_own = jnp.pad(down_weight, ((0, 8 * own_mix - units), (0, 0)))
    mixing_half = jnp.pad(mixing_half, ((0, 0), (0, rest - width // 2)))
    plane = lax.all_gather(
        jnp.concatenate([ring[:end], jnp.concatenate([down_own, mixing_half], axis=1)]),
        PLANE,
        axis=0,
    )
    gate_up_full = (
        plane[:, :end].reshape(4, 2, 2, end, wide).transpose(2, 0, 1, 3, 4)
    ).reshape(width, wide)
    mixing_half = (
        plane[:, end:, width:].reshape(4, 2, 2, 8 * own_mix, rest).transpose(2, 0, 1, 3, 4)
    ).reshape(heads * head, rest)
    mixing_other = hop(mixing_half, "c")
    mixing_full = jnp.concatenate(
        [
            jnp.where(c == 0, mixing_half, mixing_other)[:, : width // 2],
            jnp.where(c == 0, mixing_other, mixing_half)[:, : width // 2],
        ],
        axis=1,
    )
    down_full = plane[:, end : end + units_pad, :width].reshape(hidden_units, width)

    share_width = mine + head
    source = by_distance(width)
    cut = width // 4
    orders = [one_hot(width, source[n * cut : (n + 1) * cut]) for n in range(4)]
    share_full = low(sum(product(o, w[:, :share_width]) for o, w in zip(orders, chunks)))
    gains = sum(
        lax.dot_general(
            w[:, share_width:], o, (((0,), (1,)), ((), ())), preferred_element_type=jnp.float32
        )
        for o, w in zip(orders, chunks)
    )
    entry_scale, mixed_scale, middle_scale, closing_scale = (gains[k] for k in range(4))

    def positions(xs, ys, cs):
        place = ((yh ^ ys) * 4 + (x + xs) % 4) * 2 + (c ^ cs)
        return place * count + jnp.arange(count, dtype=jnp.int32)

    query_pos = jnp.concatenate([positions(0, 0, 0), positions(0, 0, 1)])
    key_pos = jnp.concatenate(
        [positions(xs, ys, cs) for cs in (0, 1) for xs in (0, 3, 1, 2) for ys in (0, 1)]
    )
    length = key_pos.shape[0]
    chip = 2 * count
    allowed = (key_pos[None, :] <= query_pos[:, None]) | (key_pos[None, :] < prefix_len[0])
    inverse = 1.0 / THETA ** (jnp.arange(half, dtype=jnp.float32) * (2.0 / head))
    angles = key_pos.astype(jnp.float32)[:, None] * inverse[None, :]
    angles = once(angles, parts[0])
    key_turn = lax.optimization_barrier((jnp.cos(angles), jnp.sin(angles)))
    turn = tuple(
        jnp.concatenate([t[:count], t[length // 2 : length // 2 + count]]) for t in key_turn
    )
    head_turn = tuple(t[:, None, :] for t in turn)

    def turned(pair):
        return (pair[0], -pair[1])


    entry_near = low(rms_scale(near.astype(jnp.float32), entry_scale))
    entry_far = low(rms_scale(far.astype(jnp.float32), entry_scale))
    ring_scale = product(low(gains), ring_order)[0]
    near_ring = low(rms_scale(near_ring.astype(jnp.float32), ring_scale))
    far_ring = low(rms_scale(far_ring.astype(jnp.float32), ring_scale))
    chip_ring = jnp.concatenate([near_ring[:count], far_ring[:count]])
    entry_chip = jnp.concatenate([entry_near[:count], entry_far[:count]])
    pair_raw = jnp.concatenate(
        [product(rows, share_full[:, mine:]) for rows in (entry_near, entry_far)]
    )
    pair = low(picked(rotate(pair_raw, *key_turn), pair_raw))
    other = hop(pair, "c")
    other = jnp.concatenate([other[length // 2 :], other[: length // 2]])
    all_keys, all_values = (picked(pair, other), picked(other, pair))
    query_raw = product(entry_chip, share_full[:, :mine])
    queries = low(rotate(query_raw.reshape(chip, heads // 2, head), *head_turn) * QSCALE)
    query_rows = queries.transpose(1, 0, 2).reshape(-1, head)

    bent = jnp.tanh(through(query_rows, all_keys) / CAP)
    expo = jnp.where(
        allowed[None], jnp.exp(CAP * bent - CAP).reshape(heads // 2, chip, length), 0.0
    ).reshape(-1, length)
    probs = expo / jnp.sum(expo, axis=1, keepdims=True)
    mixed_rows = low(product(low(probs), all_values)).reshape(heads // 2, chip, head)
    mixed_rows = mixed_rows.transpose(1, 0, 2).reshape(chip, mine)
    other_heads = hop(mixed_rows[count:], "c")
    attended = picked(
        jnp.concatenate([mixed_rows[:count], other_heads], axis=1),
        jnp.concatenate([other_heads, mixed_rows[:count]], axis=1),
    )
    inputs = tokens.astype(jnp.float32)
    incoming = cotangent.astype(jnp.float32)
    projected = product(attended, mixing_full)
    second = inputs + rms_scale(projected, mixed_scale)
    middle_in = low(rms_scale(second, middle_scale))

    def halves(values):
        cut = count // 2
        return (values[:cut], values[cut:])

    middle_parts, hiddens, gates, feeds = ([], [], [], [])
    for rows in halves(middle_in):
        middle_parts.append(ring_rows(rows))
    for parts in middle_parts:
        boths = [product(rows, gate_up_full) for rows in parts]
        gates.append([(both[:, :hidden_units], both[:, hidden_units:]) for both in boths])
        hiddens.append([low(gated(*pair)) for pair in gates[-1]])
        feeds.append(ring_sums(*(low(product(hidden, down_full)) for hidden in hiddens[-1])))
    outs, closing_terms, feed_parts, lows, middle_backs = ([], [], [], [], [])
    for feed, rows, grads in zip(feeds, halves(second), halves(incoming)):
        outs.append(low(rows + rms_scale(feed, closing_scale)))
        unused, closing_back = jax.vjp(rms_scale, feed, closing_scale)
        feed_grad, closing_term = closing_back(grads)
        closing_terms.append(closing_term)
        feed_parts.append(ring_rows(low(feed_grad)))
    layer_output = jnp.concatenate(outs)
    closing_term = sum(closing_terms)
    for parts, pairs in zip(feed_parts, gates):
        lows.append([])
        for rows, pair in zip(parts, pairs):
            unused, gated_back = jax.vjp(gated, *pair)
            gate_grad, up_grad = gated_back(through(rows, down_full))
            lows[-1].append(jnp.concatenate([low(gate_grad), low(up_grad)], axis=1))
        middle_backs.append(ring_sums(*(low(through(rows, gate_up_full)) for rows in lows[-1])))
    middle_back = jnp.concatenate(middle_backs)
    middle_parts, hiddens, feed_parts, lows = (
        [jnp.concatenate(parts) for parts in both]
        for both in (middle_parts, hiddens, feed_parts, lows)
    )
    gate_up_term = low(sum(outer(*pair) for pair in zip(middle_parts, lows)))
    down_term = low(sum(outer(*pair) for pair in zip(hiddens, feed_parts)))
    gate_up_term = gate_up_term.reshape(2, 4, 2, 8 * own, wide).transpose(1, 2, 0, 3, 4)
    down_term = jnp.pad(
        down_term.reshape(16, units_pad, width), ((0, 0), (0, 0), (0, wide - width))
    )
    plane_term = jnp.concatenate([gate_up_term.reshape(16, 8 * own, wide), down_term], axis=1)
    plane_sum = lax.psum_scatter(
        plane_term.reshape(-1, wide), PLANE, scatter_dimension=0, tiled=True
    )
    down_delta = plane_sum[8 * own : 8 * own + units, :width].astype(jnp.float32)
    gate_up_sum = lax.all_to_all(
        plane_sum[: 8 * own].reshape(8, own, wide), RING, 0, 0, tiled=True
    )
    unused, middle_vjp = jax.vjp(lambda v: rms_scale(v, middle_scale), second)
    second_part = middle_vjp(middle_back)[0]
    second_delta = incoming + second_part
    unused, mixed_vjp = jax.vjp(rms_scale, projected, mixed_scale)
    projected_grad, mixed_term = mixed_vjp(second_delta)
    projected_low = low(projected_grad)
    attended_low = low(through(projected_low, mixing_full))
    mixing_order = one_hot(heads * head, by_ring(heads * head, True))
    attended_near = low(product(attended, mixing_order))
    gain_terms = jnp.pad(jnp.stack([mixed_term, closing_term]), ((0, 6), (0, 0)))
    gain_terms = low(product(low(gain_terms), ring_order))
    back_kept = picked(attended_low[:, :mine], attended_low[:, mine:])
    back_given = picked(attended_low[:, mine:], attended_low[:, :mine])
    mixing_given = low(outer(attended_near[:, mine:], projected_low))
    back_got, mixing_got = (hop(back_given, "c"), hop(mixing_given, "c"))
    mixing_term = low(
        outer(attended_near[:, :mine], projected_low) + mixing_got.astype(jnp.float32)
    )
    back_rows = jnp.concatenate([back_kept, back_got])
    back_rows = back_rows.reshape(chip, heads // 2, head).transpose(1, 0, 2).reshape(-1, head)
    prob_back = through(back_rows, all_values)
    weighted = jnp.sum(prob_back * probs, axis=1, keepdims=True)
    capped_back = probs * (prob_back - weighted)
    score_low = low(capped_back * (1.0 - bent * bent))
    query_back = product(score_low, all_keys)
    query_grad = query_back.reshape(heads // 2, chip, head).transpose(1, 0, 2) * QSCALE
    query_low = low(rotate(query_grad, *turned(head_turn)).reshape(chip, mine))

    query_terms = quarters(low(outer(chip_ring, query_low)))
    query_terms, score_low, probs_low, back_rows = lax.optimization_barrier(
        (query_terms, score_low, low(probs), back_rows)
    )
    value_term = outer(probs_low, back_rows)
    key_term = outer(score_low, query_rows)
    given = low(picked(value_term, key_term))
    given = jnp.concatenate([given[length // 2 :], given[: length // 2]])
    cut = width // 4
    query_parts = [hop(*pair) for pair in along("x", query_terms)]
    pair_got = hop(given, "c")
    with_gains = [
        jnp.concatenate(
            [part, jnp.pad(gain_terms[:, n * cut : (n + 1) * cut], ((0, 0), (0, width - cut)))]
        )
        for n, part in enumerate(quarters(mixing_term))
    ]
    mixing_parts = [hop(*pair) for pair in along("x", with_gains)]
    pair_term = picked(key_term, value_term) + pair_got.astype(jnp.float32)
    pair_low = low(picked(rotate(pair_term, *turned(key_turn)), pair_term))
    pair_terms = quarters(
        low(
            outer(near_ring, pair_low[: length // 2]) + outer(far_ring, pair_low[length // 2 :])
        )
    )
    pair_terms, query_parts, mixing_parts = lax.optimization_barrier(
        (pair_terms, query_parts, mixing_parts)
    )
    pair_cut = low(pair_term).reshape(2, 4, -1, head)
    sums = [pair_cut[:, k].reshape(-1, head) for k in range(4)]
    *pair_parts, back, ahead, beyond = sent(
        *along("x", pair_terms), (sums[1], ("x", 3)), (sums[2], ("x", 1)), (sums[3], ("x", 2))
    )
    pair_sum = added(sums[0], (back, ahead, beyond)).reshape(2, 2, count, head)
    pair_got = hop(low(pair_sum[:, 1]), "y2")
    query_sum = added(query_terms[0], query_parts)
    mixing_sum = added(with_gains[0], mixing_parts)
    gain_columns = outer(mixing_sum[-8:, :cut], jnp.eye(8, 128, dtype=jnp.float32))
    share_sum = low(
        jnp.concatenate([query_sum, added(pair_terms[0], pair_parts), gain_columns], axis=1)
    )
    pair_own = 2 * own
    place = jnp.arange(16 * 24, dtype=jnp.int32)
    source = jnp.where(place % 24 < pair_own, place // 24 * pair_own + place % 24, -1)
    share_blocks = low(product(one_hot(cut, source, True), share_sum)).reshape(16, 24, -1)
    span = share_blocks.shape[2]
    mixing_blocks = low(mixing_sum[:-8]).reshape(16, own_mix, width)
    slack = ((0, 0), (0, 0), (0, 2 * span - width))
    plane_blocks = jnp.concatenate(
        [share_blocks, mixing_blocks[..., :span], jnp.pad(mixing_blocks[..., span:], slack)],
        axis=1,
    )
    plane_blocks, gate_up_sum = lax.optimization_barrier((plane_blocks, gate_up_sum))
    block = plane_blocks.shape[1]
    plane_parts = lax.all_to_all(
        plane_blocks.reshape(-1, span), ("yl", "z", "yh"), 0, 0, tiled=True
    )
    plane_total = jnp.sum(plane_parts.reshape(16, block, span).astype(jnp.float32), axis=0)
    share_sum = plane_total[:pair_own]
    mixing_delta = jnp.concatenate(
        [plane_total[24 : 24 + own_mix], plane_total[24 + own_mix :, : width - span]], axis=1
    )
    pair_got = once(pair_got, plane_parts)
    pair_sum = (pair_sum[:, 0] + pair_got.astype(jnp.float32)).reshape(chip, head)
    pair_low = low(picked(rotate(pair_sum, *turned(turn)), pair_sum))
    chip_back = through(jnp.concatenate([query_low, pair_low], axis=1), share_full)
    back_got = hop(low(chip_back[count:]), "c")
    share_kept, share_got = (share_sum[:own], hop(low(share_sum[own:]), "c").astype(jnp.float32))
    first = picked(share_kept, share_got)
    second_share = picked(share_got, share_kept)
    query_delta = jnp.concatenate([first[:, :mine], second_share[:, :mine]], axis=1)
    key_delta = first[:, mine:share_width]
    value_delta = second_share[:, mine:share_width]
    gain_deltas = (first + second_share)[:, share_width:]
    mixed_delta, closing_delta = (gain_deltas[:, 0], gain_deltas[:, 1])
    entry_back = chip_back[:count] + back_got.astype(jnp.float32)
    unused, entry_vjp = jax.vjp(lambda v: rms_scale(v, entry_scale), inputs)
    input_delta = second_delta + entry_vjp(entry_back)[0]

    gate_up_sum = gate_up_sum.astype(jnp.float32).reshape(8, own, 2, 4, 2, 2, units_pad)
    gate_up_sum = gate_up_sum[..., :units].transpose(2, 1, 5, 3, 4, 0, 6).reshape(2, own, -1)
    gate_delta, up_delta = (gate_up_sum[0], gate_up_sum[1])

    def gain_delta(gain, *pairs):
        total = sum(
            jnp.sum(weight.astype(jnp.float32) * delta, axis=1) for weight, delta in pairs
        )
        return total / gain.astype(jnp.float32)

    entry_delta = gain_delta(
        entry_gain,
        (
            jnp.concatenate([query_weight, key_weight, value_weight], axis=1),
            jnp.concatenate([query_delta, key_delta, value_delta], axis=1),
        ),
    )
    middle_delta = gain_delta(middle_gain, (gate_weight, gate_delta), (up_weight, up_delta))
    return (
        layer_output,
        input_delta,
        query_delta,
        key_delta,
        value_delta,
        mixing_delta,
        gate_delta,
        up_delta,
        down_delta,
        entry_delta,
        mixed_delta,
        middle_delta,
        closing_delta,
    )


def solution(mesh):
    cut = Mesh(mesh.devices.reshape(SIZES), AXES)
    rows = P(AXES, None)
    flat = P(AXES)
    in_specs = (rows, P(("yl", "z")), *(rows,) * 7, *(flat,) * 4, rows)
    out_specs = (*(rows,) * 9, *(flat,) * 4)
    return jax.shard_map(body, mesh=cut, in_specs=in_specs, out_specs=out_specs, check_vma=False)
```

```python
import jax
import jax.numpy as jnp
from jax import lax
from jax.sharding import Mesh
from jax.sharding import PartitionSpec as P

EPS = 1e-06
CAP = 20.0
QSCALE = 0.0625
THETA = 1000000.0

AXES = ("yl", "z", "yh", "x", "c")
SIZES = (2, 4, 2, 4, 2)
PLANE = ("z", "yh", "yl")
RING = ("x", "c")


def moved(step):
    pairs = []
    for yl in range(2):
        for z in range(4):
            for yh in range(2):
                for x in range(4):
                    for c in range(2):
                        to = step(yh * 2 + yl, z, x, c)
                        y2, z2, x2, c2 = (to[0] % 4, to[1] % 4, to[2] % 4, to[3] % 2)
                        here = (((yl * 4 + z) * 2 + yh) * 4 + x) * 2 + c
                        there = (((y2 % 2 * 4 + z2) * 2 + y2 // 2) * 4 + x2) * 2 + c2
                        pairs.append((here, there))
    return pairs


HOPS = {
    "c": moved(lambda y, z, x, c: (y, z, x, c + 1)),
    "y2": moved(lambda y, z, x, c: (y + 2, z, x, c)),
}
for n in (1, 2, 3):
    HOPS["x", n] = moved(lambda y, z, x, c: (y, z, x + n, c))
    HOPS["y", n] = moved(lambda y, z, x, c: (y + n, z, x, c))
    HOPS["z", n] = moved(lambda y, z, x, c: (y, z + n, x, c))


def hop(values, way):
    return lax.ppermute(values, AXES, HOPS[way])


def rms_scale(values, gain):
    return values * lax.rsqrt(jnp.mean(values * values, axis=-1, keepdims=True) + EPS) * gain


def rotate(values, cosine, sine):
    half = values.shape[-1] // 2
    first = values[..., :half]
    second = values[..., half:]
    return jnp.concatenate(
        [first * cosine - second * sine, second * cosine + first * sine], axis=-1
    )


def outer(left, right):
    return lax.dot_general(
        left, right, (((0,), (0,)), ((), ())), preferred_element_type=jnp.float32
    )


def through(left, weight):
    return lax.dot_general(
        left, weight, (((1,), (1,)), ((), ())), preferred_element_type=jnp.float32
    )


def product(left, right):
    return jnp.dot(left, right, preferred_element_type=jnp.float32)


def low(values):
    return values.astype(jnp.bfloat16)


def gated(gate, up):
    return jax.nn.gelu(gate, approximate=True) * up


def ring_rows(rows):
    near = jnp.concatenate([rows, hop(rows, ("x", 1)), hop(rows, ("x", 3)), hop(rows, ("x", 2))])
    return near, hop(near, "c")


def pair_sums(near, far):
    return low(near.astype(jnp.float32) + hop(far, "c").astype(jnp.float32))


def ring_sums(both):
    own, back, ahead, across = quarters(both)
    parts = (hop(back, ("x", 3)), hop(ahead, ("x", 1)), hop(across, ("x", 2)))
    return added(own, parts)


def stacked(parts):
    cut = parts[0].shape[0]
    rows = cut * len(parts)
    return sum(
        jnp.pad(part, ((n * cut, rows - (n + 1) * cut), (0, 0))) for n, part in enumerate(parts)
    )


def sent(*pairs):
    return lax.optimization_barrier([hop(value, way) for value, way in pairs])


def along(axis, terms):
    return [(terms[n], (axis, n)) for n in (1, 2, 3)]


def added(own, parts):
    total = own.astype(jnp.float32)
    for part in parts:
        total = total + part.astype(jnp.float32)
    return total


def quarters(values):
    cut = values.shape[0] // 4
    return [values[n * cut : (n + 1) * cut] for n in range(4)]


def once(value, *others):
    return lax.optimization_barrier((value, *others))[0]


def one_hot(rows, source, turned=False):
    place = jnp.arange(rows, dtype=jnp.int32)
    if turned:
        return low(source[:, None] == place[None, :])
    return low(place[:, None] == source[None, :])


def by_distance(size):
    here = {axis: lax.axis_index(axis) for axis in AXES}
    block = size // 128
    place = jnp.arange(size, dtype=jnp.int32)
    r, q = (place % block, place // block)
    c, z, y, x = (q, q // 2, q // 8, q // 32)
    z = (here["z"] + z) % 4
    y = (here["yh"] * 2 + here["yl"] + y) % 4
    x = (here["x"] + x) % 4
    c = (here["c"] + c) % 2
    return ((((y % 2 * 4 + z) * 2 + y // 2) * 4 + x) * 2 + c) * block + r


def by_ring(size, core_first):
    block = size // 128
    place = jnp.arange(size, dtype=jnp.int32)
    r, q = (place % block, place // block)
    if core_first:
        c, x, plane = (q // 64, q // 16, q % 16)
    else:
        c, x, plane = (q, q // 32, q // 2 % 16)
    x = (lax.axis_index("x") + x) % 4
    c = (lax.axis_index("c") + c) % 2
    return ((plane * 4 + x) * 2 + c) * block + r


def body(
    tokens,
    prefix_len,
    query_weight,
    key_weight,
    value_weight,
    mixing_weight,
    gate_weight,
    up_weight,
    down_weight,
    entry_gain,
    mixed_gain,
    middle_gain,
    closing_gain,
    cotangent,
):
    count, width = tokens.shape
    head = key_weight.shape[1]
    heads = query_weight.shape[1] // head
    half = head // 2
    own = gate_weight.shape[0]
    units = down_weight.shape[0]
    units_pad = -(-units // 8) * 8
    hidden_units = 16 * units_pad
    wide = 2 * hidden_units
    own_mix = mixing_weight.shape[0]
    x, c, yh = (lax.axis_index("x"), lax.axis_index("c"), lax.axis_index("yh"))

    def columns(weight):
        cut = weight.reshape(own, 2, 4, 2, 8, units)
        cut = jnp.pad(cut, ((0, 0),) * 5 + ((0, units_pad - units),))
        return cut.transpose(4, 0, 2, 3, 1, 5).reshape(4, 2, own, hidden_units)

    def at(values, index, axis):
        return lax.dynamic_index_in_dim(values, index, axis, keepdims=False)

    mine = heads * head // 2

    def share(core):
        queries = query_weight[:, core * mine : (core + 1) * mine]
        return jnp.concatenate([queries, (key_weight, value_weight)[core]], axis=1)

    def picked(first, second):
        return jnp.where(c == 0, first, second)

    gains_own = jnp.stack([entry_gain, mixed_gain, middle_gain, closing_gain], axis=1)
    gains_own = jnp.pad(gains_own, ((0, 0), (0, 124)))
    kept = jnp.concatenate([picked(share(0), share(1)), gains_own], axis=1)
    given = jnp.concatenate([picked(share(1), share(0)), gains_own], axis=1)
    gate_up = jnp.concatenate([columns(gate_weight), columns(up_weight)], axis=3)
    mixing_own = jnp.pad(mixing_weight, ((0, 0), (0, wide - width)))

    swapped = hop(
        jnp.concatenate([at(gate_up, 1 - c, 1).reshape(4 * own, wide), mixing_own]), "c"
    )
    blocks = hop(given, "c")
    pair_up = jnp.concatenate(
        [at(gate_up, c, 1), swapped[: 4 * own].reshape(4, own, wide)], axis=1
    )
    pair_mixing = jnp.concatenate([mixing_own, swapped[4 * own :]])
    ring = [jnp.concatenate([at(pair_up, (x + n) % 4, 0), pair_mixing]) for n in range(4)]
    *parts, across = sent(*along("x", ring), (tokens, "y2"))
    ring = jnp.concatenate([ring[0], *parts])
    blocks = jnp.concatenate([kept, blocks])
    near = jnp.concatenate([tokens, across])
    near, blocks, ring = lax.optimization_barrier((near, blocks, ring))
    back, ahead, *parts = sent(
        (near, ("x", 1)), (near, ("x", 3)), *((blocks, ("z", n)) for n in (3, 2, 1))
    )
    blocks = stacked([blocks, *parts])
    over, under, *parts = sent(
        (back[:count], ("x", 1)),
        (ahead[count:], ("x", 3)),
        *((blocks, ("y", n)) for n in (3, 2, 1)),
    )
    near = jnp.concatenate([near, back, ahead, over, under])
    blocks = stacked([blocks, *parts])
    far = hop(near, "c")
    chip_rows = jnp.concatenate([tokens, hop(tokens, "c")])
    chunks = [blocks, *(hop(blocks, ("x", n)) for n in (3, 2, 1))]
    def positions(xs, ys, cs):
        place = ((yh ^ ys) * 4 + (x + xs) % 4) * 2 + (c ^ cs)
        return place * count + jnp.arange(count, dtype=jnp.int32)

    query_pos = jnp.concatenate([positions(0, 0, 0), positions(0, 0, 1)])
    key_pos = jnp.concatenate(
        [positions(xs, ys, cs) for cs in (0, 1) for xs in (0, 3, 1, 2) for ys in (0, 1)]
    )
    length = key_pos.shape[0]
    chip = 2 * count
    allowed = (key_pos[None, :] <= query_pos[:, None]) | (key_pos[None, :] < prefix_len[0])
    inverse = 1.0 / THETA ** (jnp.arange(half, dtype=jnp.float32) * (2.0 / head))
    angles = key_pos.astype(jnp.float32)[:, None] * inverse[None, :]
    angles = once(angles, over)
    key_turn = lax.optimization_barrier((jnp.cos(angles), jnp.sin(angles)))
    ring_order = one_hot(width, by_ring(width, False))
    chunks, near_ring, far_ring, chip_ring = lax.optimization_barrier(
        (chunks, *(low(product(rows, ring_order)) for rows in (near, far, chip_rows)))
    )
    turn = tuple(
        jnp.concatenate([t[:count], t[length // 2 : length // 2 + count]]) for t in key_turn
    )
    head_turn = tuple(t[:, None, :] for t in turn)

    step = 2 * (own + own_mix)
    place = jnp.arange(4 * step, dtype=jnp.int32)
    q, r = (place // own, place % own)
    up_source = (x - q // 2) % 4 * step + (q % 2 ^ c) * own + r
    q, r = ((place - 8 * own) // own_mix, (place - 8 * own) % own_mix)
    mixing_source = (x - q // 2) % 4 * step + 2 * own + (q % 2 ^ c) * own_mix + r
    source = jnp.where(place < 8 * own, up_source, mixing_source)
    ring = low(outer(one_hot(4 * step, source), ring))
    end = 8 * own
    rest = wide - width
    mixing_half = ring[end:, : width // 2]
    mixing_half = jnp.where(c == 0, mixing_half, ring[end:, width // 2 : width])
    down_own = jnp.pad(down_weight, ((0, 8 * own_mix - units), (0, 0)))
    mixing_half = jnp.pad(mixing_half, ((0, 0), (0, rest - width // 2)))
    plane = lax.all_gather(
        jnp.concatenate([ring[:end], jnp.concatenate([down_own, mixing_half], axis=1)]),
        PLANE,
        axis=0,
    )
    gate_up_full = (
        plane[:, :end].reshape(4, 2, 2, end, wide).transpose(2, 0, 1, 3, 4)
    ).reshape(width, wide)
    mixing_half = plane[:, end:, width:].reshape(-1, rest)
    mixing_other = hop(mixing_half, "c")
    mixing_full = jnp.concatenate(
        [
            jnp.where(c == 0, mixing_half, mixing_other)[:, : width // 2],
            jnp.where(c == 0, mixing_other, mixing_half)[:, : width // 2],
        ],
        axis=1,
    )
    mixing_full = mixing_full.reshape(4, 2, 2, 8 * own_mix, width).transpose(2, 0, 1, 3, 4)
    mixing_full = mixing_full.reshape(heads * head, width)
    down_full = plane[:, end : end + units_pad, :width].reshape(hidden_units, width)

    share_width = mine + head
    order = one_hot(width, by_distance(width))
    share_full = low(product(order, jnp.concatenate([w[:, :share_width] for w in chunks])))
    gains = lax.dot_general(
        jnp.concatenate([w[:, share_width:] for w in chunks]),
        order,
        (((0,), (1,)), ((), ())),
        preferred_element_type=jnp.float32,
    )
    entry_scale, mixed_scale, middle_scale, closing_scale = (gains[k] for k in range(4))

    def turned(pair):
        return (pair[0], -pair[1])


    def scale_of(rows):
        rows = rows.astype(jnp.float32)
        return lax.rsqrt(jnp.mean(rows * rows, axis=-1, keepdims=True) + EPS)

    def normed(rows, scale):
        return low(rows.astype(jnp.float32) * scale * entry_scale)

    near_scale, far_scale, chip_scale = (scale_of(rows) for rows in (near, far, chip_rows))
    pair_raw = jnp.concatenate(
        [
            product(normed(near, near_scale), share_full[:, mine:]),
            product(normed(far, far_scale), share_full[:, mine:]),
        ]
    )
    pair = low(picked(rotate(pair_raw, *key_turn), pair_raw))
    other = hop(pair, "c")
    other = jnp.concatenate([other[length // 2 :], other[: length // 2]])
    all_keys, all_values = (picked(pair, other), picked(other, pair))
    query_raw = product(normed(chip_rows, chip_scale), share_full[:, :mine])
    queries = low(rotate(query_raw.reshape(chip, heads // 2, head), *head_turn) * QSCALE)
    query_rows = queries.transpose(1, 0, 2).reshape(-1, head)

    bent = jnp.tanh(through(query_rows, all_keys) / CAP)
    expo = jnp.where(
        allowed[None], jnp.exp(CAP * bent - CAP).reshape(heads // 2, chip, length), 0.0
    ).reshape(-1, length)
    probs = expo / jnp.sum(expo, axis=1, keepdims=True)
    mixed_rows = low(product(low(probs), all_values)).reshape(heads // 2, chip, head)
    mixed_rows = mixed_rows.transpose(1, 0, 2).reshape(chip, mine)
    other_heads = hop(mixed_rows[count:], "c")
    attended = picked(
        jnp.concatenate([mixed_rows[:count], other_heads], axis=1),
        jnp.concatenate([other_heads, mixed_rows[:count]], axis=1),
    )
    inputs = tokens.astype(jnp.float32)
    incoming = cotangent.astype(jnp.float32)
    projected = product(attended, mixing_full)
    second = inputs + rms_scale(projected, mixed_scale)
    middle_in = low(rms_scale(second, middle_scale))

    middle_parts = ring_rows(middle_in)
    gates, hiddens = ([], [])
    for rows in middle_parts:
        both = product(rows, gate_up_full)
        gates.append((both[:, :hidden_units], both[:, hidden_units:]))
        hiddens.append(low(gated(*gates[-1])))
    feed = ring_sums(pair_sums(*(low(product(hidden, down_full)) for hidden in hiddens)))
    layer_output = low(second + rms_scale(feed, closing_scale))

    unused, closing_back = jax.vjp(rms_scale, feed, closing_scale)
    feed_grad, closing_term = closing_back(incoming)
    feed_parts = ring_rows(low(feed_grad))
    lows = []
    for rows, pair in zip(feed_parts, gates):
        unused, gated_back = jax.vjp(gated, *pair)
        gate_grad, up_grad = gated_back(through(rows, down_full))
        lows.append(jnp.concatenate([low(gate_grad), low(up_grad)], axis=1))
    both = pair_sums(*(low(through(rows, gate_up_full)) for rows in lows))
    both, *rows_of = lax.optimization_barrier((both, middle_parts, hiddens, feed_parts, lows))
    middle_back = ring_sums(both)
    middle_rows, hidden_rows, feed_rows, low_rows = (jnp.concatenate(parts) for parts in rows_of)
    gate_up_term = low(outer(middle_rows, low_rows))
    down_term = low(outer(hidden_rows, feed_rows))
    gate_up_term = gate_up_term.reshape(2, 4, 2, 8 * own, wide).transpose(1, 2, 0, 3, 4)
    down_term = jnp.pad(
        down_term.reshape(16, units_pad, width), ((0, 0), (0, 0), (0, wide - width))
    )
    plane_term = jnp.concatenate([gate_up_term.reshape(16, 8 * own, wide), down_term], axis=1)
    plane_sum = lax.psum_scatter(
        plane_term.reshape(-1, wide), PLANE, scatter_dimension=0, tiled=True
    )
    down_delta = plane_sum[8 * own : 8 * own + units, :width].astype(jnp.float32)
    tall = 16
    place = jnp.arange(8 * tall, dtype=jnp.int32)
    q, r = (place // tall, place % tall)
    source = ((x + q // 2) % 4 * 2 + (c + q) % 2) * own + r
    source = jnp.where(r < own, source, -1)
    ring = quarters(low(product(one_hot(8 * own, source, True), plane_sum[: 8 * own])))
    ring = [ring[0], *(hop(*pair) for pair in along("x", ring))]
    unused, middle_vjp = jax.vjp(lambda v: rms_scale(v, middle_scale), second)
    second_part = middle_vjp(middle_back)[0]
    second_delta = incoming + second_part
    unused, mixed_vjp = jax.vjp(rms_scale, projected, mixed_scale)
    projected_grad, mixed_term = mixed_vjp(second_delta)
    projected_low = low(projected_grad)
    attended_low = low(through(projected_low, mixing_full))
    mixing_order = one_hot(heads * head, by_ring(heads * head, True))
    attended_near = low(product(attended, mixing_order))
    gain_terms = jnp.pad(jnp.stack([mixed_term, closing_term]), ((0, 6), (0, 0)))
    gain_terms = low(product(low(gain_terms), ring_order))
    back_kept = picked(attended_low[:, :mine], attended_low[:, mine:])
    back_given = picked(attended_low[:, mine:], attended_low[:, :mine])
    mixing_given = low(outer(attended_near[:, mine:], projected_low))
    back_got, mixing_got = (hop(back_given, "c"), hop(mixing_given, "c"))
    mixing_term = low(
        outer(attended_near[:, :mine], projected_low) + mixing_got.astype(jnp.float32)
    )
    back_rows = jnp.concatenate([back_kept, back_got])
    back_rows = back_rows.reshape(chip, heads // 2, head).transpose(1, 0, 2).reshape(-1, head)
    prob_back = through(back_rows, all_values)
    weighted = jnp.sum(prob_back * probs, axis=1, keepdims=True)
    capped_back = probs * (prob_back - weighted)
    score_low = low(capped_back * (1.0 - bent * bent))
    query_back = product(score_low, all_keys)
    query_grad = query_back.reshape(heads // 2, chip, head).transpose(1, 0, 2) * QSCALE
    query_grad = rotate(query_grad, *turned(head_turn)).reshape(chip, mine)
    query_low = low(query_grad)

    query_terms = quarters(low(outer(chip_ring, low(query_grad * chip_scale))))
    query_terms, score_low, probs_low, back_rows = lax.optimization_barrier(
        (query_terms, score_low, low(probs), back_rows)
    )
    value_term = outer(probs_low, back_rows)
    key_term = outer(score_low, query_rows)
    given = low(picked(value_term, key_term))
    given = jnp.concatenate([given[length // 2 :], given[: length // 2]])
    cut = width // 4
    query_parts = [hop(*pair) for pair in along("x", query_terms)]
    pair_got = hop(given, "c")
    with_gains = [
        jnp.concatenate(
            [part, jnp.pad(gain_terms[:, n * cut : (n + 1) * cut], ((0, 0), (0, width - cut)))]
        )
        for n, part in enumerate(quarters(mixing_term))
    ]
    mixing_parts = [hop(*pair) for pair in along("x", with_gains)]
    pair_term = picked(key_term, value_term) + pair_got.astype(jnp.float32)
    pair_low = picked(rotate(pair_term, *turned(key_turn)), pair_term)
    pair_terms = quarters(
        low(
            outer(near_ring, low(pair_low[: length // 2] * near_scale))
            + outer(far_ring, low(pair_low[length // 2 :] * far_scale))
        )
    )
    pair_terms, query_parts = lax.optimization_barrier((pair_terms, query_parts))
    pair_parts = [hop(*pair) for pair in along("x", pair_terms)]
    pair_cut, pair_parts, mixing_parts = lax.optimization_barrier(
        (low(pair_term), pair_parts, mixing_parts)
    )
    pair_cut = pair_cut.reshape(2, 4, -1, head)
    sums = [pair_cut[:, k].reshape(-1, head) for k in range(4)]
    back, ahead, beyond = (hop(sums[1], ("x", 3)), hop(sums[2], ("x", 1)), hop(sums[3], ("x", 2)))
    pair_sum = added(sums[0], (back, ahead, beyond)).reshape(2, 2, count, head)
    query_sum = added(query_terms[0], query_parts)
    mixing_sum = added(with_gains[0], mixing_parts)
    gain_columns = outer(mixing_sum[-8:, :cut], jnp.eye(8, 128, dtype=jnp.float32))
    share_sum = low(
        jnp.concatenate([query_sum, added(pair_terms[0], pair_parts), gain_columns], axis=1)
    )
    pair_own = 2 * own
    place = jnp.arange(16 * 24, dtype=jnp.int32)
    source = jnp.where(place % 24 < pair_own, place // 24 * pair_own + place % 24, -1)
    share_blocks = low(product(one_hot(cut, source, True), share_sum)).reshape(16, 24, -1)
    span = share_blocks.shape[2]
    mixing_blocks = low(mixing_sum[:-8]).reshape(16, own_mix, width)
    slack = ((0, 0), (0, 0), (0, 2 * span - width))
    plane_blocks = jnp.concatenate(
        [share_blocks, mixing_blocks[..., :span], jnp.pad(mixing_blocks[..., span:], slack)],
        axis=1,
    )
    block = plane_blocks.shape[1]
    plane_parts = lax.all_to_all(
        plane_blocks.reshape(-1, span), ("yl", "z", "yh"), 0, 0, tiled=True
    )
    ring, pair_sum = lax.optimization_barrier((ring, pair_sum))
    ring_got = hop(jnp.concatenate([part[tall:] for part in ring]), "c")
    ring = jnp.concatenate([part[:tall] for part in ring] + [ring_got])
    place = jnp.arange(8 * own, dtype=jnp.int32)
    q, r = (place // own, place % own)
    source = (c + q) % 2 * 4 * tall + (x - q // 2) % 4 * tall + r
    gate_up_sum = product(one_hot(8 * tall, source, True), ring)
    gate_up_sum = gate_up_sum.reshape(8, own, 2, 4, 2, 2, units_pad)
    gate_up_sum = gate_up_sum[..., :units].transpose(2, 1, 5, 3, 4, 0, 6).reshape(2, own, -1)
    pair_got = hop(low(pair_sum[:, 1]), "y2")
    pair_sum = (pair_sum[:, 0] + pair_got.astype(jnp.float32)).reshape(chip, head)
    pair_low = low(picked(rotate(pair_sum, *turned(turn)), pair_sum))
    chip_back = through(jnp.concatenate([query_low, pair_low], axis=1), share_full)
    back_got = hop(low(chip_back[count:]), "c")
    plane_parts, gate_up_sum, back_got = lax.optimization_barrier(
        (plane_parts, gate_up_sum, back_got)
    )
    plane_total = jnp.sum(plane_parts.reshape(16, block, span).astype(jnp.float32), axis=0)
    share_sum = plane_total[:pair_own]
    mixing_delta = jnp.concatenate(
        [plane_total[24 : 24 + own_mix], plane_total[24 + own_mix :, : width - span]], axis=1
    )
    share_kept, share_got = (share_sum[:own], hop(low(share_sum[own:]), "c").astype(jnp.float32))
    first = picked(share_kept, share_got)
    second_share = picked(share_got, share_kept)
    share_delta = jnp.concatenate(
        [
            first[:, :mine],
            second_share[:, :mine],
            first[:, mine:share_width],
            second_share[:, mine:share_width],
        ],
        axis=1,
    )
    entry_delta = jnp.sum(
        jnp.concatenate([query_weight, key_weight, value_weight], axis=1) * share_delta, axis=1
    )
    share_delta = share_delta * entry_gain.astype(jnp.float32)[:, None]
    query_delta, key_delta, value_delta = jnp.split(
        share_delta, [2 * mine, 2 * mine + head], axis=1
    )
    gain_deltas = (first + second_share)[:, share_width:]
    mixed_delta, closing_delta = (gain_deltas[:, 0], gain_deltas[:, 1])
    entry_back = chip_back[:count] + back_got.astype(jnp.float32)
    unused, entry_vjp = jax.vjp(lambda v: rms_scale(v, entry_scale), inputs)
    input_delta = second_delta + entry_vjp(entry_back)[0]

    gate_delta, up_delta = (gate_up_sum[0], gate_up_sum[1])

    def gain_delta(gain, *pairs):
        total = sum(
            jnp.sum(weight.astype(jnp.float32) * delta, axis=1) for weight, delta in pairs
        )
        return total / gain.astype(jnp.float32)

    middle_delta = gain_delta(middle_gain, (gate_weight, gate_delta), (up_weight, up_delta))
    return (
        layer_output,
        input_delta,
        query_delta,
        key_delta,
        value_delta,
        mixing_delta,
        gate_delta,
        up_delta,
        down_delta,
        entry_delta,
        mixed_delta,
        middle_delta,
        closing_delta,
    )


def solution(mesh):
    cut = Mesh(mesh.devices.reshape(SIZES), AXES)
    rows = P(AXES, None)
    flat = P(AXES)
    in_specs = (rows, P(("yl", "z")), *(rows,) * 7, *(flat,) * 4, rows)
    out_specs = (*(rows,) * 9, *(flat,) * 4)
    return jax.shard_map(body, mesh=cut, in_specs=in_specs, out_specs=out_specs, check_vma=False)
```

```python
import jax
import jax.numpy as jnp
from jax import lax
from jax.sharding import Mesh
from jax.sharding import PartitionSpec as P

EPS = 1e-06
CAP = 20.0
QSCALE = 0.0625
THETA = 1000000.0

AXES = ("yl", "z", "yh", "x", "c")
SIZES = (2, 4, 2, 4, 2)
PLANE = ("z", "yh", "yl")
RING = ("x", "c")


def moved(step):
    pairs = []
    for yl in range(2):
        for z in range(4):
            for yh in range(2):
                for x in range(4):
                    for c in range(2):
                        to = step(yh * 2 + yl, z, x, c)
                        y2, z2, x2, c2 = (to[0] % 4, to[1] % 4, to[2] % 4, to[3] % 2)
                        here = (((yl * 4 + z) * 2 + yh) * 4 + x) * 2 + c
                        there = (((y2 % 2 * 4 + z2) * 2 + y2 // 2) * 4 + x2) * 2 + c2
                        pairs.append((here, there))
    return pairs


HOPS = {
    "c": moved(lambda y, z, x, c: (y, z, x, c + 1)),
    "y2": moved(lambda y, z, x, c: (y + 2, z, x, c)),
}
for n in (1, 2, 3):
    HOPS["x", n] = moved(lambda y, z, x, c: (y, z, x + n, c))
    HOPS["y", n] = moved(lambda y, z, x, c: (y + n, z, x, c))
    HOPS["z", n] = moved(lambda y, z, x, c: (y, z + n, x, c))


def hop(values, way):
    return lax.ppermute(values, AXES, HOPS[way])


def rms_scale(values, gain):
    return values * lax.rsqrt(jnp.mean(values * values, axis=-1, keepdims=True) + EPS) * gain


def rotate(values, cosine, sine):
    half = values.shape[-1] // 2
    first = values[..., :half]
    second = values[..., half:]
    return jnp.concatenate(
        [first * cosine - second * sine, second * cosine + first * sine], axis=-1
    )


def outer(left, right):
    return lax.dot_general(
        left, right, (((0,), (0,)), ((), ())), preferred_element_type=jnp.float32
    )


def through(left, weight):
    return lax.dot_general(
        left, weight, (((1,), (1,)), ((), ())), preferred_element_type=jnp.float32
    )


def product(left, right):
    return jnp.dot(left, right, preferred_element_type=jnp.float32)


def low(values):
    return values.astype(jnp.bfloat16)


def gated(gate, up):
    return jax.nn.gelu(gate, approximate=True) * up


def ring_rows(rows):
    near = jnp.concatenate([rows, hop(rows, ("x", 1)), hop(rows, ("x", 3)), hop(rows, ("x", 2))])
    return near, hop(near, "c")


def pair_sums(near, far):
    return low(near.astype(jnp.float32) + hop(far, "c").astype(jnp.float32))


def ring_sums(both):
    own, back, ahead, across = quarters(both)
    parts = (hop(back, ("x", 3)), hop(ahead, ("x", 1)), hop(across, ("x", 2)))
    return added(own, parts)


def stacked(parts):
    cut = parts[0].shape[0]
    rows = cut * len(parts)
    return sum(
        jnp.pad(part, ((n * cut, rows - (n + 1) * cut), (0, 0))) for n, part in enumerate(parts)
    )


def sent(*pairs):
    return lax.optimization_barrier([hop(value, way) for value, way in pairs])


def along(axis, terms):
    return [(terms[n], (axis, n)) for n in (1, 2, 3)]


def added(own, parts):
    total = own.astype(jnp.float32)
    for part in parts:
        total = total + part.astype(jnp.float32)
    return total


def quarters(values):
    cut = values.shape[0] // 4
    return [values[n * cut : (n + 1) * cut] for n in range(4)]


def once(value, *others):
    return lax.optimization_barrier((value, *others))[0]


def one_hot(rows, source, turned=False):
    place = jnp.arange(rows, dtype=jnp.int32)
    if turned:
        return low(source[:, None] == place[None, :])
    return low(place[:, None] == source[None, :])


def by_distance(size):
    here = {axis: lax.axis_index(axis) for axis in AXES}
    block = size // 128
    place = jnp.arange(size, dtype=jnp.int32)
    r, q = (place % block, place // block)
    c, z, y, x = (q, q // 2, q // 8, q // 32)
    z = (here["z"] + z) % 4
    y = (here["yh"] * 2 + here["yl"] + y) % 4
    x = (here["x"] + x) % 4
    c = (here["c"] + c) % 2
    return ((((y % 2 * 4 + z) * 2 + y // 2) * 4 + x) * 2 + c) * block + r


def by_ring(size, core_first):
    block = size // 128
    place = jnp.arange(size, dtype=jnp.int32)
    r, q = (place % block, place // block)
    if core_first:
        c, x, plane = (q // 64, q // 16, q % 16)
    else:
        c, x, plane = (q, q // 32, q // 2 % 16)
    x = (lax.axis_index("x") + x) % 4
    c = (lax.axis_index("c") + c) % 2
    return ((plane * 4 + x) * 2 + c) * block + r


def body(
    tokens,
    prefix_len,
    query_weight,
    key_weight,
    value_weight,
    mixing_weight,
    gate_weight,
    up_weight,
    down_weight,
    entry_gain,
    mixed_gain,
    middle_gain,
    closing_gain,
    cotangent,
):
    count, width = tokens.shape
    head = key_weight.shape[1]
    heads = query_weight.shape[1] // head
    half = head // 2
    own = gate_weight.shape[0]
    units = down_weight.shape[0]
    units_pad = -(-units // 8) * 8
    hidden_units = 16 * units_pad
    wide = 2 * hidden_units
    own_mix = mixing_weight.shape[0]
    x, c, yh = (lax.axis_index("x"), lax.axis_index("c"), lax.axis_index("yh"))

    def columns(weight):
        cut = weight.reshape(own, 2, 4, 2, 8, units)
        cut = jnp.pad(cut, ((0, 0),) * 5 + ((0, units_pad - units),))
        return cut.transpose(4, 0, 2, 3, 1, 5).reshape(4, 2, own, hidden_units)

    def at(values, index, axis):
        return lax.dynamic_index_in_dim(values, index, axis, keepdims=False)

    mine = heads * head // 2

    def share(core):
        queries = query_weight[:, core * mine : (core + 1) * mine]
        return jnp.concatenate([queries, (key_weight, value_weight)[core]], axis=1)

    def picked(first, second):
        return jnp.where(c == 0, first, second)

    gains_own = jnp.stack([entry_gain, mixed_gain, middle_gain, closing_gain], axis=1)
    gains_own = jnp.pad(gains_own, ((0, 0), (0, 124)))
    kept = jnp.concatenate([picked(share(0), share(1)), gains_own], axis=1)
    given = jnp.concatenate([picked(share(1), share(0)), gains_own], axis=1)
    gate_up = jnp.concatenate([columns(gate_weight), columns(up_weight)], axis=3)
    mixing_own = jnp.pad(mixing_weight, ((0, 0), (0, wide - width)))

    swapped = hop(
        jnp.concatenate([at(gate_up, 1 - c, 1).reshape(4 * own, wide), mixing_own]), "c"
    )
    blocks = hop(given, "c")
    pair_up = jnp.concatenate(
        [at(gate_up, c, 1), swapped[: 4 * own].reshape(4, own, wide)], axis=1
    )
    pair_mixing = jnp.concatenate([mixing_own, swapped[4 * own :]])
    ring = [jnp.concatenate([at(pair_up, (x + n) % 4, 0), pair_mixing]) for n in range(4)]
    blocks = jnp.concatenate([kept, blocks])
    *parts, across = sent(
        *along("x", ring), *((blocks, ("z", n)) for n in (3, 2, 1)), (tokens, "y2")
    )
    ring = jnp.concatenate([ring[0], *parts[:3]])
    blocks = stacked([blocks, *parts[3:]])
    near = jnp.concatenate([tokens, across])
    near, blocks, ring = lax.optimization_barrier((near, blocks, ring))
    back, ahead = sent((near, ("x", 1)), (near, ("x", 3)))
    blocks, back, ahead = lax.optimization_barrier((blocks, back, ahead))
    over, under, *parts = sent(
        (back[:count], ("x", 1)),
        (ahead[count:], ("x", 3)),
        *((blocks, ("y", n)) for n in (3, 2, 1)),
    )
    near = jnp.concatenate([near, back, ahead, over, under])
    blocks = stacked([blocks, *parts])
    far = hop(near, "c")
    chip_rows = jnp.concatenate([tokens, hop(tokens, "c")])
    chunks = [blocks, *(hop(blocks, ("x", n)) for n in (3, 2, 1))]
    def positions(xs, ys, cs):
        place = ((yh ^ ys) * 4 + (x + xs) % 4) * 2 + (c ^ cs)
        return place * count + jnp.arange(count, dtype=jnp.int32)

    query_pos = jnp.concatenate([positions(0, 0, 0), positions(0, 0, 1)])
    key_pos = jnp.concatenate(
        [positions(xs, ys, cs) for cs in (0, 1) for xs in (0, 3, 1, 2) for ys in (0, 1)]
    )
    length = key_pos.shape[0]
    chip = 2 * count
    allowed = (key_pos[None, :] <= query_pos[:, None]) | (key_pos[None, :] < prefix_len[0])
    inverse = 1.0 / THETA ** (jnp.arange(half, dtype=jnp.float32) * (2.0 / head))
    angles = key_pos.astype(jnp.float32)[:, None] * inverse[None, :]
    angles = once(angles, over)
    key_turn = lax.optimization_barrier((jnp.cos(angles), jnp.sin(angles)))
    ring_order = one_hot(width, by_ring(width, False))
    chunks, near_ring, far_ring, chip_ring = lax.optimization_barrier(
        (chunks, *(low(product(rows, ring_order)) for rows in (near, far, chip_rows)))
    )
    turn = tuple(
        jnp.concatenate([t[:count], t[length // 2 : length // 2 + count]]) for t in key_turn
    )
    head_turn = tuple(t[:, None, :] for t in turn)

    step = 2 * (own + own_mix)
    place = jnp.arange(4 * step, dtype=jnp.int32)
    q, r = (place // own, place % own)
    up_source = (x - q // 2) % 4 * step + (q % 2 ^ c) * own + r
    q, r = ((place - 8 * own) // own_mix, (place - 8 * own) % own_mix)
    mixing_source = (x - q // 2) % 4 * step + 2 * own + (q % 2 ^ c) * own_mix + r
    source = jnp.where(place < 8 * own, up_source, mixing_source)
    ring = low(outer(one_hot(4 * step, source), ring))
    end = 8 * own
    rest = wide - width
    mixing_half = ring[end:, : width // 2]
    mixing_half = jnp.where(c == 0, mixing_half, ring[end:, width // 2 : width])
    down_own = jnp.pad(down_weight, ((0, 8 * own_mix - units), (0, 0)))
    mixing_half = jnp.pad(mixing_half, ((0, 0), (0, rest - width // 2)))
    plane = lax.all_gather(
        jnp.concatenate([ring[:end], jnp.concatenate([down_own, mixing_half], axis=1)]),
        PLANE,
        axis=0,
    )
    gate_up_full = (
        plane[:, :end].reshape(4, 2, 2, end, wide).transpose(2, 0, 1, 3, 4)
    ).reshape(width, wide)
    mixing_half = plane[:, end:, width:].reshape(-1, rest)
    mixing_other = hop(mixing_half, "c")
    mixing_full = jnp.concatenate(
        [
            jnp.where(c == 0, mixing_half, mixing_other)[:, : width // 2],
            jnp.where(c == 0, mixing_other, mixing_half)[:, : width // 2],
        ],
        axis=1,
    )
    mixing_full = mixing_full.reshape(4, 2, 2, 8 * own_mix, width).transpose(2, 0, 1, 3, 4)
    mixing_full = mixing_full.reshape(heads * head, width)
    down_full = plane[:, end : end + units_pad, :width].reshape(hidden_units, width)

    share_width = mine + head
    order = one_hot(width, by_distance(width))
    share_full = low(product(order, jnp.concatenate([w[:, :share_width] for w in chunks])))
    gains = lax.dot_general(
        jnp.concatenate([w[:, share_width:] for w in chunks]),
        order,
        (((0,), (1,)), ((), ())),
        preferred_element_type=jnp.float32,
    )
    entry_scale, mixed_scale, middle_scale, closing_scale = (gains[k] for k in range(4))

    def turned(pair):
        return (pair[0], -pair[1])


    def scale_of(rows):
        rows = rows.astype(jnp.float32)
        return lax.rsqrt(jnp.mean(rows * rows, axis=-1, keepdims=True) + EPS)

    def normed(rows, scale):
        return low(rows.astype(jnp.float32) * scale * entry_scale)

    near_scale, far_scale, chip_scale = (scale_of(rows) for rows in (near, far, chip_rows))
    pair_raw = jnp.concatenate(
        [
            product(normed(near, near_scale), share_full[:, mine:]),
            product(normed(far, far_scale), share_full[:, mine:]),
        ]
    )
    pair = low(picked(rotate(pair_raw, *key_turn), pair_raw))
    other = hop(pair, "c")
    other = jnp.concatenate([other[length // 2 :], other[: length // 2]])
    all_keys, all_values = (picked(pair, other), picked(other, pair))
    query_raw = product(normed(chip_rows, chip_scale), share_full[:, :mine])
    queries = low(rotate(query_raw.reshape(chip, heads // 2, head), *head_turn) * QSCALE)
    query_rows = queries.transpose(1, 0, 2).reshape(-1, head)

    bent = jnp.tanh(through(query_rows, all_keys) / CAP)
    expo = jnp.where(
        allowed[None], jnp.exp(CAP * bent - CAP).reshape(heads // 2, chip, length), 0.0
    ).reshape(-1, length)
    probs = expo / jnp.sum(expo, axis=1, keepdims=True)
    mixed_rows = low(product(low(probs), all_values)).reshape(heads // 2, chip, head)
    mixed_rows = mixed_rows.transpose(1, 0, 2).reshape(chip, mine)
    other_heads = hop(mixed_rows[count:], "c")
    attended = picked(
        jnp.concatenate([mixed_rows[:count], other_heads], axis=1),
        jnp.concatenate([other_heads, mixed_rows[:count]], axis=1),
    )
    inputs = tokens.astype(jnp.float32)
    incoming = cotangent.astype(jnp.float32)
    projected = product(attended, mixing_full)
    second = inputs + rms_scale(projected, mixed_scale)
    middle_in = low(rms_scale(second, middle_scale))

    middle_parts = ring_rows(middle_in)
    gates, hiddens = ([], [])
    for rows in middle_parts:
        both = product(rows, gate_up_full)
        gates.append((both[:, :hidden_units], both[:, hidden_units:]))
        hiddens.append(low(gated(*gates[-1])))
    feed = ring_sums(pair_sums(*(low(product(hidden, down_full)) for hidden in hiddens)))
    layer_output = low(second + rms_scale(feed, closing_scale))

    unused, closing_back = jax.vjp(rms_scale, feed, closing_scale)
    feed_grad, closing_term = closing_back(incoming)
    feed_parts = ring_rows(low(feed_grad))
    lows = []
    for rows, pair in zip(feed_parts, gates):
        unused, gated_back = jax.vjp(gated, *pair)
        gate_grad, up_grad = gated_back(through(rows, down_full))
        lows.append(jnp.concatenate([low(gate_grad), low(up_grad)], axis=1))
    both = pair_sums(*(low(through(rows, gate_up_full)) for rows in lows))
    both, *rows_of = lax.optimization_barrier((both, middle_parts, hiddens, feed_parts, lows))
    middle_back = ring_sums(both)
    middle_rows, hidden_rows, feed_rows, low_rows = (jnp.concatenate(parts) for parts in rows_of)
    gate_up_term = low(outer(middle_rows, low_rows))
    down_term = low(outer(hidden_rows, feed_rows))
    gate_up_term = gate_up_term.reshape(2, 4, 2, 8 * own, wide).transpose(1, 2, 0, 3, 4)
    down_term = jnp.pad(
        down_term.reshape(16, units_pad, width), ((0, 0), (0, 0), (0, wide - width))
    )
    plane_term = jnp.concatenate([gate_up_term.reshape(16, 8 * own, wide), down_term], axis=1)
    plane_sum = lax.psum_scatter(
        plane_term.reshape(-1, wide), PLANE, scatter_dimension=0, tiled=True
    )
    down_delta = plane_sum[8 * own : 8 * own + units, :width].astype(jnp.float32)
    tall = 16
    place = jnp.arange(8 * tall, dtype=jnp.int32)
    q, r = (place // tall, place % tall)
    source = ((x + q // 2) % 4 * 2 + (c + q) % 2) * own + r
    source = jnp.where(r < own, source, -1)
    ring = quarters(low(product(one_hot(8 * own, source, True), plane_sum[: 8 * own])))
    ring = [ring[0], *(hop(*pair) for pair in along("x", ring))]
    unused, middle_vjp = jax.vjp(lambda v: rms_scale(v, middle_scale), second)
    second_part = middle_vjp(middle_back)[0]
    second_delta = incoming + second_part
    unused, mixed_vjp = jax.vjp(rms_scale, projected, mixed_scale)
    projected_grad, mixed_term = mixed_vjp(second_delta)
    projected_low = low(projected_grad)
    attended_low = low(through(projected_low, mixing_full))
    mixing_order = one_hot(heads * head, by_ring(heads * head, True))
    attended_near = low(product(attended, mixing_order))
    gain_terms = jnp.pad(jnp.stack([mixed_term, closing_term]), ((0, 6), (0, 0)))
    gain_terms = low(product(low(gain_terms), ring_order))
    back_kept = picked(attended_low[:, :mine], attended_low[:, mine:])
    back_given = picked(attended_low[:, mine:], attended_low[:, :mine])
    mixing_given = low(outer(attended_near[:, mine:], projected_low))
    back_got, mixing_got = (hop(back_given, "c"), hop(mixing_given, "c"))
    mixing_term = low(
        outer(attended_near[:, :mine], projected_low) + mixing_got.astype(jnp.float32)
    )
    back_rows = jnp.concatenate([back_kept, back_got])
    back_rows = back_rows.reshape(chip, heads // 2, head).transpose(1, 0, 2).reshape(-1, head)
    prob_back = through(back_rows, all_values)
    weighted = jnp.sum(prob_back * probs, axis=1, keepdims=True)
    capped_back = probs * (prob_back - weighted)
    score_low = low(capped_back * (1.0 - bent * bent))
    query_back = product(score_low, all_keys)
    query_grad = query_back.reshape(heads // 2, chip, head).transpose(1, 0, 2) * QSCALE
    query_grad = rotate(query_grad, *turned(head_turn)).reshape(chip, mine)
    query_low = low(query_grad)

    query_terms = quarters(low(outer(chip_ring, low(query_grad * chip_scale))))
    query_terms, score_low, probs_low, back_rows = lax.optimization_barrier(
        (query_terms, score_low, low(probs), back_rows)
    )
    value_term = outer(probs_low, back_rows)
    key_term = outer(score_low, query_rows)
    given = low(picked(value_term, key_term))
    given = jnp.concatenate([given[length // 2 :], given[: length // 2]])
    cut = width // 4
    query_parts = [hop(*pair) for pair in along("x", query_terms)]
    pair_got = hop(given, "c")
    with_gains = [
        jnp.concatenate(
            [part, jnp.pad(gain_terms[:, n * cut : (n + 1) * cut], ((0, 0), (0, width - cut)))]
        )
        for n, part in enumerate(quarters(mixing_term))
    ]
    mixing_parts = [hop(*pair) for pair in along("x", with_gains)]
    pair_term = picked(key_term, value_term) + pair_got.astype(jnp.float32)
    pair_low = picked(rotate(pair_term, *turned(key_turn)), pair_term)
    pair_terms = quarters(
        low(
            outer(near_ring, low(pair_low[: length // 2] * near_scale))
            + outer(far_ring, low(pair_low[length // 2 :] * far_scale))
        )
    )
    pair_terms, query_parts = lax.optimization_barrier((pair_terms, query_parts))
    pair_parts = [hop(*pair) for pair in along("x", pair_terms)]
    pair_cut, pair_parts, mixing_parts = lax.optimization_barrier(
        (low(pair_term), pair_parts, mixing_parts)
    )
    pair_cut = pair_cut.reshape(2, 4, -1, head)
    sums = [pair_cut[:, k].reshape(-1, head) for k in range(4)]
    back, ahead, beyond = (hop(sums[1], ("x", 3)), hop(sums[2], ("x", 1)), hop(sums[3], ("x", 2)))
    pair_sum = added(sums[0], (back, ahead, beyond)).reshape(2, 2, count, head)
    query_sum = added(query_terms[0], query_parts)
    mixing_sum = added(with_gains[0], mixing_parts)
    gain_columns = outer(mixing_sum[-8:, :cut], jnp.eye(8, 128, dtype=jnp.float32))
    share_sum = low(
        jnp.concatenate([query_sum, added(pair_terms[0], pair_parts), gain_columns], axis=1)
    )
    pair_own = 2 * own
    place = jnp.arange(16 * 24, dtype=jnp.int32)
    source = jnp.where(place % 24 < pair_own, place // 24 * pair_own + place % 24, -1)
    share_blocks = low(product(one_hot(cut, source, True), share_sum)).reshape(16, 24, -1)
    span = share_blocks.shape[2]
    mixing_blocks = low(mixing_sum[:-8]).reshape(16, own_mix, width)
    slack = ((0, 0), (0, 0), (0, 2 * span - width))
    plane_blocks = jnp.concatenate(
        [share_blocks, mixing_blocks[..., :span], jnp.pad(mixing_blocks[..., span:], slack)],
        axis=1,
    )
    block = plane_blocks.shape[1]
    plane_parts = lax.all_to_all(
        plane_blocks.reshape(-1, span), ("yl", "z", "yh"), 0, 0, tiled=True
    )
    ring[0], pair_sum = lax.optimization_barrier((ring[0], pair_sum))
    ring = jnp.concatenate(ring)
    ring_got = hop(ring, "c")
    place = jnp.arange(8 * own, dtype=jnp.int32)
    q, r = (place // own, place % own)
    source = (x - q // 2) % 4 * 2 * tall + r
    other = (c + q) % 2 == 1
    gate_up_sum = product(
        one_hot(8 * tall, jnp.where(other, -1, source), True), ring
    ) + product(one_hot(8 * tall, jnp.where(other, source + tall, -1), True), ring_got)
    gate_up_sum = gate_up_sum.reshape(8, own, 2, 4, 2, 2, units_pad)
    gate_up_sum = gate_up_sum[..., :units].transpose(2, 1, 5, 3, 4, 0, 6).reshape(2, own, -1)
    pair_got = hop(low(pair_sum[:, 1]), "y2")
    pair_sum = (pair_sum[:, 0] + pair_got.astype(jnp.float32)).reshape(chip, head)
    pair_low = low(picked(rotate(pair_sum, *turned(turn)), pair_sum))
    chip_back = through(jnp.concatenate([query_low, pair_low], axis=1), share_full)
    back_got = hop(low(chip_back[count:]), "c")
    plane_parts, gate_up_sum, back_got = lax.optimization_barrier(
        (plane_parts, gate_up_sum, back_got)
    )
    plane_total = jnp.sum(plane_parts.reshape(16, block, span).astype(jnp.float32), axis=0)
    share_sum = plane_total[:pair_own]
    mixing_delta = jnp.concatenate(
        [plane_total[24 : 24 + own_mix], plane_total[24 + own_mix :, : width - span]], axis=1
    )
    share_kept, share_got = (share_sum[:own], hop(low(share_sum[own:]), "c").astype(jnp.float32))
    first = picked(share_kept, share_got)
    second_share = picked(share_got, share_kept)
    share_delta = jnp.concatenate(
        [
            first[:, :mine],
            second_share[:, :mine],
            first[:, mine:share_width],
            second_share[:, mine:share_width],
        ],
        axis=1,
    )
    entry_delta = jnp.sum(
        jnp.concatenate([query_weight, key_weight, value_weight], axis=1) * share_delta, axis=1
    )
    share_delta = share_delta * entry_gain.astype(jnp.float32)[:, None]
    query_delta, key_delta, value_delta = jnp.split(
        share_delta, [2 * mine, 2 * mine + head], axis=1
    )
    gain_deltas = (first + second_share)[:, share_width:]
    mixed_delta, closing_delta = (gain_deltas[:, 0], gain_deltas[:, 1])
    entry_back = chip_back[:count] + back_got.astype(jnp.float32)
    unused, entry_vjp = jax.vjp(lambda v: rms_scale(v, entry_scale), inputs)
    input_delta = second_delta + entry_vjp(entry_back)[0]

    gate_delta, up_delta = (gate_up_sum[0], gate_up_sum[1])

    def gain_delta(gain, *pairs):
        total = sum(
            jnp.sum(weight.astype(jnp.float32) * delta, axis=1) for weight, delta in pairs
        )
        return total / gain.astype(jnp.float32)

    middle_delta = gain_delta(middle_gain, (gate_weight, gate_delta), (up_weight, up_delta))
    return (
        layer_output,
        input_delta,
        query_delta,
        key_delta,
        value_delta,
        mixing_delta,
        gate_delta,
        up_delta,
        down_delta,
        entry_delta,
        mixed_delta,
        middle_delta,
        closing_delta,
    )


def solution(mesh):
    cut = Mesh(mesh.devices.reshape(SIZES), AXES)
    rows = P(AXES, None)
    flat = P(AXES)
    in_specs = (rows, P(("yl", "z")), *(rows,) * 7, *(flat,) * 4, rows)
    out_specs = (*(rows,) * 9, *(flat,) * 4)
    return jax.shard_map(body, mesh=cut, in_specs=in_specs, out_specs=out_specs, check_vma=False)
```

```python
import jax
import jax.numpy as jnp
from jax import lax
from jax.sharding import Mesh
from jax.sharding import PartitionSpec as P

EPS = 1e-06
CAP = 20.0
QSCALE = 0.0625
THETA = 1000000.0

AXES = ("yl", "z", "yh", "x", "c")
SIZES = (2, 4, 2, 4, 2)
PLANE = ("z", "yh", "yl")
RING = ("x", "c")


def moved(step):
    pairs = []
    for yl in range(2):
        for z in range(4):
            for yh in range(2):
                for x in range(4):
                    for c in range(2):
                        to = step(yh * 2 + yl, z, x, c)
                        y2, z2, x2, c2 = (to[0] % 4, to[1] % 4, to[2] % 4, to[3] % 2)
                        here = (((yl * 4 + z) * 2 + yh) * 4 + x) * 2 + c
                        there = (((y2 % 2 * 4 + z2) * 2 + y2 // 2) * 4 + x2) * 2 + c2
                        pairs.append((here, there))
    return pairs


HOPS = {
    "c": moved(lambda y, z, x, c: (y, z, x, c + 1)),
    "y2": moved(lambda y, z, x, c: (y + 2, z, x, c)),
}
for n in (1, 2, 3):
    HOPS["x", n] = moved(lambda y, z, x, c: (y, z, x + n, c))
    HOPS["y", n] = moved(lambda y, z, x, c: (y + n, z, x, c))
    HOPS["z", n] = moved(lambda y, z, x, c: (y, z + n, x, c))


def hop(values, way):
    return lax.ppermute(values, AXES, HOPS[way])


def rms_scale(values, gain):
    return values * lax.rsqrt(jnp.mean(values * values, axis=-1, keepdims=True) + EPS) * gain


def rotate(values, cosine, sine):
    half = values.shape[-1] // 2
    first = values[..., :half]
    second = values[..., half:]
    return jnp.concatenate(
        [first * cosine - second * sine, second * cosine + first * sine], axis=-1
    )


def outer(left, right):
    return lax.dot_general(
        left, right, (((0,), (0,)), ((), ())), preferred_element_type=jnp.float32
    )


def through(left, weight):
    return lax.dot_general(
        left, weight, (((1,), (1,)), ((), ())), preferred_element_type=jnp.float32
    )


def product(left, right):
    return jnp.dot(left, right, preferred_element_type=jnp.float32)


def low(values):
    return values.astype(jnp.bfloat16)


def gated(gate, up):
    return jax.nn.gelu(gate, approximate=True) * up


def ring_rows(rows):
    near = jnp.concatenate([rows, hop(rows, ("x", 1)), hop(rows, ("x", 3)), hop(rows, ("x", 2))])
    return near, hop(near, "c")


def pair_sums(near, far):
    return low(near.astype(jnp.float32) + hop(far, "c").astype(jnp.float32))


def ring_sums(both):
    own, back, ahead, across = quarters(both)
    parts = (hop(back, ("x", 3)), hop(ahead, ("x", 1)), hop(across, ("x", 2)))
    return added(own, parts)


def stacked(parts):
    cut = parts[0].shape[0]
    rows = cut * len(parts)
    return sum(
        jnp.pad(part, ((n * cut, rows - (n + 1) * cut), (0, 0))) for n, part in enumerate(parts)
    )


def sent(*pairs):
    return lax.optimization_barrier([hop(value, way) for value, way in pairs])


def along(axis, terms):
    return [(terms[n], (axis, n)) for n in (1, 2, 3)]


def added(own, parts):
    total = own.astype(jnp.float32)
    for part in parts:
        total = total + part.astype(jnp.float32)
    return total


def quarters(values):
    cut = values.shape[0] // 4
    return [values[n * cut : (n + 1) * cut] for n in range(4)]


def once(value, *others):
    return lax.optimization_barrier((value, *others))[0]


def one_hot(rows, source, turned=False):
    place = jnp.arange(rows, dtype=jnp.int32)
    if turned:
        return low(source[:, None] == place[None, :])
    return low(place[:, None] == source[None, :])


def by_distance(size):
    here = {axis: lax.axis_index(axis) for axis in AXES}
    block = size // 128
    place = jnp.arange(size, dtype=jnp.int32)
    r, q = (place % block, place // block)
    c, z, y, x = (q, q // 2, q // 8, q // 32)
    z = (here["z"] + z) % 4
    y = (here["yh"] * 2 + here["yl"] + y) % 4
    x = (here["x"] + x) % 4
    c = (here["c"] + c) % 2
    return ((((y % 2 * 4 + z) * 2 + y // 2) * 4 + x) * 2 + c) * block + r


def by_ring(size, core_first):
    block = size // 128
    place = jnp.arange(size, dtype=jnp.int32)
    r, q = (place % block, place // block)
    if core_first:
        c, x, plane = (q // 64, q // 16, q % 16)
    else:
        c, x, plane = (q, q // 32, q // 2 % 16)
    x = (lax.axis_index("x") + x) % 4
    c = (lax.axis_index("c") + c) % 2
    return ((plane * 4 + x) * 2 + c) * block + r


def body(
    tokens,
    prefix_len,
    query_weight,
    key_weight,
    value_weight,
    mixing_weight,
    gate_weight,
    up_weight,
    down_weight,
    entry_gain,
    mixed_gain,
    middle_gain,
    closing_gain,
    cotangent,
):
    count, width = tokens.shape
    head = key_weight.shape[1]
    heads = query_weight.shape[1] // head
    half = head // 2
    own = gate_weight.shape[0]
    units = down_weight.shape[0]
    units_pad = -(-units // 8) * 8
    hidden_units = 16 * units_pad
    wide = 2 * hidden_units
    own_mix = mixing_weight.shape[0]
    x, c, yh = (lax.axis_index("x"), lax.axis_index("c"), lax.axis_index("yh"))

    def columns(weight):
        cut = weight.reshape(own, 2, 4, 2, 8, units)
        cut = jnp.pad(cut, ((0, 0),) * 5 + ((0, units_pad - units),))
        return cut.transpose(4, 0, 2, 3, 1, 5).reshape(4, 2, own, hidden_units)

    def at(values, index, axis):
        return lax.dynamic_index_in_dim(values, index, axis, keepdims=False)

    mine = heads * head // 2

    def share(core):
        queries = query_weight[:, core * mine : (core + 1) * mine]
        return jnp.concatenate([queries, (key_weight, value_weight)[core]], axis=1)

    def picked(first, second):
        return jnp.where(c == 0, first, second)

    gains_own = jnp.stack([entry_gain, mixed_gain, middle_gain, closing_gain], axis=1)
    gains_own = jnp.pad(gains_own, ((0, 0), (0, 124)))
    kept = jnp.concatenate([picked(share(0), share(1)), gains_own], axis=1)
    given = jnp.concatenate([picked(share(1), share(0)), gains_own], axis=1)
    gate_up = jnp.concatenate([columns(gate_weight), columns(up_weight)], axis=3)
    mixing_own = jnp.pad(mixing_weight, ((0, 0), (0, wide - width)))

    swapped = hop(
        jnp.concatenate([at(gate_up, 1 - c, 1).reshape(4 * own, wide), mixing_own]), "c"
    )
    blocks = hop(given, "c")
    pair_up = jnp.concatenate(
        [at(gate_up, c, 1), swapped[: 4 * own].reshape(4, own, wide)], axis=1
    )
    pair_mixing = jnp.concatenate([mixing_own, swapped[4 * own :]])
    ring = [jnp.concatenate([at(pair_up, (x + n) % 4, 0), pair_mixing]) for n in range(4)]
    blocks = jnp.concatenate([kept, blocks])
    *parts, across = sent(
        *along("x", ring), *((blocks, ("z", n)) for n in (3, 2, 1)), (tokens, "y2")
    )
    ring = jnp.concatenate([ring[0], *parts[:3]])
    blocks = stacked([blocks, *parts[3:]])
    near = jnp.concatenate([tokens, across])
    near, blocks, ring = lax.optimization_barrier((near, blocks, ring))
    back, ahead = sent((near, ("x", 1)), (near, ("x", 3)))
    blocks, back, ahead = lax.optimization_barrier((blocks, back, ahead))
    over, under, *parts = sent(
        (back[:count], ("x", 1)),
        (ahead[count:], ("x", 3)),
        *((blocks, ("y", n)) for n in (3, 2, 1)),
    )
    near = jnp.concatenate([near, back, ahead, over, under])
    blocks = stacked([blocks, *parts])
    far = hop(near, "c")
    chip_rows = jnp.concatenate([tokens, hop(tokens, "c")])
    chunks = [blocks, *(hop(blocks, ("x", n)) for n in (3, 2, 1))]
    def positions(xs, ys, cs):
        place = ((yh ^ ys) * 4 + (x + xs) % 4) * 2 + (c ^ cs)
        return place * count + jnp.arange(count, dtype=jnp.int32)

    query_pos = jnp.concatenate([positions(0, 0, 0), positions(0, 0, 1)])
    key_pos = jnp.concatenate(
        [positions(xs, ys, cs) for cs in (0, 1) for xs in (0, 3, 1, 2) for ys in (0, 1)]
    )
    length = key_pos.shape[0]
    chip = 2 * count
    allowed = (key_pos[None, :] <= query_pos[:, None]) | (key_pos[None, :] < prefix_len[0])
    inverse = 1.0 / THETA ** (jnp.arange(half, dtype=jnp.float32) * (2.0 / head))
    angles = key_pos.astype(jnp.float32)[:, None] * inverse[None, :]
    angles = once(angles, over)
    key_turn = lax.optimization_barrier((jnp.cos(angles), jnp.sin(angles)))
    ring_order = one_hot(width, by_ring(width, False))
    chunks, near_ring, far_ring, chip_ring = lax.optimization_barrier(
        (chunks, *(low(product(rows, ring_order)) for rows in (near, far, chip_rows)))
    )
    turn = tuple(
        jnp.concatenate([t[:count], t[length // 2 : length // 2 + count]]) for t in key_turn
    )

    step = 2 * (own + own_mix)
    place = jnp.arange(4 * step, dtype=jnp.int32)
    q, r = (place // own, place % own)
    up_source = (x - q // 2) % 4 * step + (q % 2 ^ c) * own + r
    q, r = ((place - 8 * own) // own_mix, (place - 8 * own) % own_mix)
    mixing_source = (x - q // 2) % 4 * step + 2 * own + (q % 2 ^ c) * own_mix + r
    source = jnp.where(place < 8 * own, up_source, mixing_source)
    ring = low(outer(one_hot(4 * step, source), ring))
    end = 8 * own
    rest = wide - width
    mixing_half = jnp.where(
        c == 0, ring[end:, :rest], jnp.pad(ring[end:, rest:width], ((0, 0), (0, 2 * rest - width)))
    )
    down_own = jnp.pad(down_weight, ((0, 8 * own_mix - units), (0, 0)))
    plane = lax.all_gather(
        jnp.concatenate([ring[:end], jnp.concatenate([down_own, mixing_half], axis=1)]),
        PLANE,
        axis=0,
    )
    gate_up_full = (
        plane[:, :end].reshape(4, 2, 2, end, wide).transpose(2, 0, 1, 3, 4)
    ).reshape(width, wide)
    mixing_half = plane[:, end:, width:].reshape(-1, rest)
    mixing_other = hop(mixing_half, "c")
    mixing_full = jnp.concatenate(
        [
            jnp.where(c == 0, mixing_half, mixing_other),
            jnp.where(c == 0, mixing_other, mixing_half)[:, : width - rest],
        ],
        axis=1,
    )
    mixing_full = mixing_full.reshape(4, 2, 2, 8 * own_mix, width).transpose(2, 0, 1, 3, 4)
    mixing_full = mixing_full.reshape(heads * head, width)
    down_full = plane[:, end : end + units_pad, :width].reshape(hidden_units, width)

    share_width = mine + head
    order = one_hot(width, by_distance(width))
    share_full = low(product(order, jnp.concatenate([w[:, :share_width] for w in chunks])))
    gains = lax.dot_general(
        jnp.concatenate([w[:, share_width:] for w in chunks]),
        order,
        (((0,), (1,)), ((), ())),
        preferred_element_type=jnp.float32,
    )
    entry_scale, mixed_scale, middle_scale, closing_scale = (gains[k] for k in range(4))

    def turned(pair):
        return (pair[0], -pair[1])


    def scale_of(rows):
        rows = rows.astype(jnp.float32)
        return lax.rsqrt(jnp.mean(rows * rows, axis=-1, keepdims=True) + EPS)

    def normed(rows, scale):
        return low(rows.astype(jnp.float32) * scale * entry_scale)

    near_scale, far_scale, chip_scale = (scale_of(rows) for rows in (near, far, chip_rows))
    pair_raw = jnp.concatenate(
        [
            product(normed(near, near_scale), share_full[:, mine:]),
            product(normed(far, far_scale), share_full[:, mine:]),
        ]
    )
    pair = low(picked(rotate(pair_raw, *key_turn), pair_raw))
    other = hop(pair, "c")
    other = jnp.concatenate([other[length // 2 :], other[: length // 2]])
    all_keys, all_values = (picked(pair, other), picked(other, pair))
    query_raw = product(normed(chip_rows, chip_scale), share_full[:, :mine])
    query_rows = jnp.concatenate(
        [low(rotate(part, *turn) * QSCALE) for part in jnp.split(query_raw, heads // 2, axis=1)]
    )

    bent = jnp.tanh(through(query_rows, all_keys) / CAP)
    expo = jnp.where(
        allowed[None], jnp.exp(CAP * bent - CAP).reshape(heads // 2, chip, length), 0.0
    ).reshape(-1, length)
    probs = expo / jnp.sum(expo, axis=1, keepdims=True)
    mixed_rows = low(product(low(probs), all_values))
    mixed_rows = jnp.concatenate(jnp.split(mixed_rows, heads // 2), axis=1)
    other_heads = hop(mixed_rows[count:], "c")
    attended = picked(
        jnp.concatenate([mixed_rows[:count], other_heads], axis=1),
        jnp.concatenate([other_heads, mixed_rows[:count]], axis=1),
    )
    inputs = tokens.astype(jnp.float32)
    incoming = cotangent.astype(jnp.float32)
    projected = product(attended, mixing_full)
    second = inputs + rms_scale(projected, mixed_scale)
    middle_in = low(rms_scale(second, middle_scale))

    middle_parts = ring_rows(middle_in)
    gates, hiddens = ([], [])
    for rows in middle_parts:
        both = product(rows, gate_up_full)
        gates.append((both[:, :hidden_units], both[:, hidden_units:]))
        hiddens.append(low(gated(*gates[-1])))
    feed = ring_sums(pair_sums(*(low(product(hidden, down_full)) for hidden in hiddens)))
    layer_output = low(second + rms_scale(feed, closing_scale))

    unused, closing_back = jax.vjp(rms_scale, feed, closing_scale)
    feed_grad, closing_term = closing_back(incoming)
    feed_parts = ring_rows(low(feed_grad))
    lows = []
    for rows, pair in zip(feed_parts, gates):
        unused, gated_back = jax.vjp(gated, *pair)
        gate_grad, up_grad = gated_back(through(rows, down_full))
        lows.append(jnp.concatenate([low(gate_grad), low(up_grad)], axis=1))
    both = pair_sums(*(low(through(rows, gate_up_full)) for rows in lows))
    both, *rows_of = lax.optimization_barrier((both, middle_parts, hiddens, feed_parts, lows))
    middle_back = ring_sums(both)
    middle_rows, hidden_rows, feed_rows, low_rows = (jnp.concatenate(parts) for parts in rows_of)
    gate_up_term = low(outer(middle_rows, low_rows))
    down_term = low(outer(hidden_rows, feed_rows))
    gate_up_term = gate_up_term.reshape(2, 4, 2, 8 * own, wide).transpose(1, 2, 0, 3, 4)
    down_term = jnp.pad(
        down_term.reshape(16, units_pad, width), ((0, 0), (0, 0), (0, wide - width))
    )
    plane_term = jnp.concatenate([gate_up_term.reshape(16, 8 * own, wide), down_term], axis=1)
    plane_sum = lax.psum_scatter(
        plane_term.reshape(-1, wide), PLANE, scatter_dimension=0, tiled=True
    )
    down_delta = plane_sum[8 * own : 8 * own + units, :width].astype(jnp.float32)
    tall = 16
    place = jnp.arange(8 * tall, dtype=jnp.int32)
    q, r = (place // tall, place % tall)
    source = ((x + q // 2) % 4 * 2 + (c + q) % 2) * own + r
    source = jnp.where(r < own, source, -1)
    ring = quarters(low(product(one_hot(8 * own, source, True), plane_sum[: 8 * own])))
    ring = [ring[0], *(hop(*pair) for pair in along("x", ring))]
    unused, middle_vjp = jax.vjp(lambda v: rms_scale(v, middle_scale), second)
    second_part = middle_vjp(middle_back)[0]
    second_delta = incoming + second_part
    unused, mixed_vjp = jax.vjp(rms_scale, projected, mixed_scale)
    projected_grad, mixed_term = mixed_vjp(second_delta)
    projected_low = low(projected_grad)
    attended_low = low(through(projected_low, mixing_full))
    mixing_order = one_hot(heads * head, by_ring(heads * head, True))
    attended_near = low(product(attended, mixing_order))
    gain_terms = jnp.pad(jnp.stack([mixed_term, closing_term]), ((0, 6), (0, 0)))
    gain_terms = low(product(low(gain_terms), ring_order))
    back_kept = picked(attended_low[:, :mine], attended_low[:, mine:])
    back_given = picked(attended_low[:, mine:], attended_low[:, :mine])
    mixing_given = low(outer(attended_near[:, mine:], projected_low))
    back_got, mixing_got = (hop(back_given, "c"), hop(mixing_given, "c"))
    mixing_term = low(
        outer(attended_near[:, :mine], projected_low) + mixing_got.astype(jnp.float32)
    )
    back_rows = jnp.concatenate([back_kept, back_got])
    back_rows = jnp.concatenate(jnp.split(back_rows, heads // 2, axis=1))
    prob_back = through(back_rows, all_values)
    weighted = jnp.sum(prob_back * probs, axis=1, keepdims=True)
    capped_back = probs * (prob_back - weighted)
    score_low = low(capped_back * (1.0 - bent * bent))
    query_back = product(score_low, all_keys)
    query_grad = jnp.concatenate(
        [
            rotate(part * QSCALE, *turned(turn))
            for part in jnp.split(query_back, heads // 2)
        ],
        axis=1,
    )
    query_low = low(query_grad)

    query_terms = quarters(low(outer(chip_ring, low(query_grad * chip_scale))))
    query_terms, score_low, probs_low, back_rows = lax.optimization_barrier(
        (query_terms, score_low, low(probs), back_rows)
    )
    value_term = outer(probs_low, back_rows)
    key_term = outer(score_low, query_rows)
    given = low(picked(value_term, key_term))
    given = jnp.concatenate([given[length // 2 :], given[: length // 2]])
    cut = width // 4
    query_parts = [hop(*pair) for pair in along("x", query_terms)]
    pair_got = hop(given, "c")
    with_gains = [
        jnp.concatenate(
            [part, jnp.pad(gain_terms[:, n * cut : (n + 1) * cut], ((0, 0), (0, width - cut)))]
        )
        for n, part in enumerate(quarters(mixing_term))
    ]
    mixing_parts = [hop(*pair) for pair in along("x", with_gains)]
    pair_term = picked(key_term, value_term) + pair_got.astype(jnp.float32)
    pair_low = picked(rotate(pair_term, *turned(key_turn)), pair_term)
    pair_terms = quarters(
        low(
            outer(near_ring, low(pair_low[: length // 2] * near_scale))
            + outer(far_ring, low(pair_low[length // 2 :] * far_scale))
        )
    )
    pair_terms, query_parts = lax.optimization_barrier((pair_terms, query_parts))
    pair_parts = [hop(*pair) for pair in along("x", pair_terms)]
    pair_cut, pair_parts, mixing_parts = lax.optimization_barrier(
        (low(pair_term), pair_parts, mixing_parts)
    )
    pair_cut = pair_cut.reshape(2, 4, -1, head)
    sums = [pair_cut[:, k].reshape(-1, head) for k in range(4)]
    back, ahead, beyond = (hop(sums[1], ("x", 3)), hop(sums[2], ("x", 1)), hop(sums[3], ("x", 2)))
    pair_sum = added(sums[0], (back, ahead, beyond)).reshape(2, 2, count, head)
    query_sum = added(query_terms[0], query_parts)
    mixing_sum = added(with_gains[0], mixing_parts)
    gain_columns = outer(mixing_sum[-8:, :cut], jnp.eye(8, 128, dtype=jnp.float32))
    share_sum = low(
        jnp.concatenate([query_sum, added(pair_terms[0], pair_parts), gain_columns], axis=1)
    )
    pair_own = 2 * own
    place = jnp.arange(16 * 24, dtype=jnp.int32)
    source = jnp.where(place % 24 < pair_own, place // 24 * pair_own + place % 24, -1)
    share_blocks = low(product(one_hot(cut, source, True), share_sum)).reshape(16, 24, -1)
    span = share_blocks.shape[2]
    mixing_blocks = low(mixing_sum[:-8]).reshape(16, own_mix, width)
    slack = ((0, 0), (0, 0), (0, 2 * span - width))
    plane_blocks = jnp.concatenate(
        [share_blocks, mixing_blocks[..., :span], jnp.pad(mixing_blocks[..., span:], slack)],
        axis=1,
    )
    block = plane_blocks.shape[1]
    plane_parts = lax.all_to_all(
        plane_blocks.reshape(-1, span), ("yl", "z", "yh"), 0, 0, tiled=True
    )
    ring[0], pair_sum = lax.optimization_barrier((ring[0], pair_sum))
    ring = stacked(ring)
    ring_got = hop(ring, "c")
    place = jnp.arange(8 * own, dtype=jnp.int32)
    q, r = (place // own, place % own)
    source = (x - q // 2) % 4 * 2 * tall + r
    other = (c + q) % 2 == 1
    gate_up_sum = product(
        one_hot(8 * tall, jnp.where(other, -1, source), True), ring
    ) + product(one_hot(8 * tall, jnp.where(other, source + tall, -1), True), ring_got)
    gate_up_sum = gate_up_sum.reshape(8, own, 2, 4, 2, 2, units_pad)
    gate_up_sum = gate_up_sum[..., :units].transpose(2, 1, 5, 3, 4, 0, 6).reshape(2, own, -1)
    pair_got = hop(low(pair_sum[:, 1]), "y2")
    pair_sum = (pair_sum[:, 0] + pair_got.astype(jnp.float32)).reshape(chip, head)
    pair_low = low(picked(rotate(pair_sum, *turned(turn)), pair_sum))
    chip_back = through(jnp.concatenate([query_low, pair_low], axis=1), share_full)
    back_got = hop(low(chip_back[count:]), "c")
    plane_parts, gate_up_sum, back_got = lax.optimization_barrier(
        (plane_parts, gate_up_sum, back_got)
    )
    plane_total = jnp.sum(plane_parts.reshape(16, block, span).astype(jnp.float32), axis=0)
    share_sum = plane_total[:pair_own]
    mixing_delta = jnp.concatenate(
        [plane_total[24 : 24 + own_mix], plane_total[24 + own_mix :, : width - span]], axis=1
    )
    share_kept, share_got = (share_sum[:own], hop(low(share_sum[own:]), "c").astype(jnp.float32))
    first = picked(share_kept, share_got)
    second_share = picked(share_got, share_kept)
    share_delta = jnp.concatenate(
        [
            first[:, :mine],
            second_share[:, :mine],
            first[:, mine:share_width],
            second_share[:, mine:share_width],
        ],
        axis=1,
    )
    entry_delta = jnp.sum(
        jnp.concatenate([query_weight, key_weight, value_weight], axis=1) * share_delta, axis=1
    )
    share_delta = share_delta * entry_gain.astype(jnp.float32)[:, None]
    query_delta, key_delta, value_delta = jnp.split(
        share_delta, [2 * mine, 2 * mine + head], axis=1
    )
    gain_deltas = (first + second_share)[:, share_width:]
    mixed_delta, closing_delta = (gain_deltas[:, 0], gain_deltas[:, 1])
    entry_back = chip_back[:count] + back_got.astype(jnp.float32)
    unused, entry_vjp = jax.vjp(lambda v: rms_scale(v, entry_scale), inputs)
    input_delta = second_delta + entry_vjp(entry_back)[0]

    gate_delta, up_delta = (gate_up_sum[0], gate_up_sum[1])

    def gain_delta(gain, *pairs):
        total = sum(
            jnp.sum(weight.astype(jnp.float32) * delta, axis=1) for weight, delta in pairs
        )
        return total / gain.astype(jnp.float32)

    middle_delta = gain_delta(middle_gain, (gate_weight, gate_delta), (up_weight, up_delta))
    return (
        layer_output,
        input_delta,
        query_delta,
        key_delta,
        value_delta,
        mixing_delta,
        gate_delta,
        up_delta,
        down_delta,
        entry_delta,
        mixed_delta,
        middle_delta,
        closing_delta,
    )


def solution(mesh):
    cut = Mesh(mesh.devices.reshape(SIZES), AXES)
    rows = P(AXES, None)
    flat = P(AXES)
    in_specs = (rows, P(("yl", "z")), *(rows,) * 7, *(flat,) * 4, rows)
    out_specs = (*(rows,) * 9, *(flat,) * 4)
    return jax.shard_map(body, mesh=cut, in_specs=in_specs, out_specs=out_specs, check_vma=False)
```

```python
import jax
import jax.numpy as jnp
from jax import lax
from jax.sharding import Mesh
from jax.sharding import PartitionSpec as P

EPS = 1e-06
CAP = 20.0
QSCALE = 0.0625
THETA = 1000000.0

AXES = ("yl", "z", "yh", "x", "c")
SIZES = (2, 4, 2, 4, 2)
PLANE = ("z", "yh", "yl")
RING = ("x", "c")


def moved(step):
    pairs = []
    for yl in range(2):
        for z in range(4):
            for yh in range(2):
                for x in range(4):
                    for c in range(2):
                        to = step(yh * 2 + yl, z, x, c)
                        y2, z2, x2, c2 = (to[0] % 4, to[1] % 4, to[2] % 4, to[3] % 2)
                        here = (((yl * 4 + z) * 2 + yh) * 4 + x) * 2 + c
                        there = (((y2 % 2 * 4 + z2) * 2 + y2 // 2) * 4 + x2) * 2 + c2
                        pairs.append((here, there))
    return pairs


HOPS = {
    "c": moved(lambda y, z, x, c: (y, z, x, c + 1)),
    "y2": moved(lambda y, z, x, c: (y + 2, z, x, c)),
}
for n in (1, 2, 3):
    HOPS["x", n] = moved(lambda y, z, x, c: (y, z, x + n, c))
    HOPS["y", n] = moved(lambda y, z, x, c: (y + n, z, x, c))
    HOPS["z", n] = moved(lambda y, z, x, c: (y, z + n, x, c))


def hop(values, way):
    return lax.ppermute(values, AXES, HOPS[way])


def rms_scale(values, gain):
    return values * lax.rsqrt(jnp.mean(values * values, axis=-1, keepdims=True) + EPS) * gain


def rotate(values, cosine, sine):
    half = values.shape[-1] // 2
    first = values[..., :half]
    second = values[..., half:]
    return jnp.concatenate(
        [first * cosine - second * sine, second * cosine + first * sine], axis=-1
    )


def outer(left, right):
    return lax.dot_general(
        left, right, (((0,), (0,)), ((), ())), preferred_element_type=jnp.float32
    )


def through(left, weight):
    return lax.dot_general(
        left, weight, (((1,), (1,)), ((), ())), preferred_element_type=jnp.float32
    )


def product(left, right):
    return jnp.dot(left, right, preferred_element_type=jnp.float32)


def low(values):
    return values.astype(jnp.bfloat16)


def gated(gate, up):
    return jax.nn.gelu(gate, approximate=True) * up


def ring_rows(rows):
    near = jnp.concatenate([rows, hop(rows, ("x", 1)), hop(rows, ("x", 3)), hop(rows, ("x", 2))])
    return near, hop(near, "c")


def pair_sums(near, far):
    return low(near.astype(jnp.float32) + hop(far, "c").astype(jnp.float32))


def ring_sums(both):
    own, back, ahead, across = quarters(both)
    parts = (hop(back, ("x", 3)), hop(ahead, ("x", 1)), hop(across, ("x", 2)))
    return added(own, parts)


def stacked(parts):
    cut = parts[0].shape[0]
    rows = cut * len(parts)
    return sum(
        jnp.pad(part, ((n * cut, rows - (n + 1) * cut), (0, 0))) for n, part in enumerate(parts)
    )


def sent(*pairs):
    return lax.optimization_barrier([hop(value, way) for value, way in pairs])


def along(axis, terms):
    return [(terms[n], (axis, n)) for n in (1, 2, 3)]


def added(own, parts):
    total = own.astype(jnp.float32)
    for part in parts:
        total = total + part.astype(jnp.float32)
    return total


def quarters(values):
    cut = values.shape[0] // 4
    return [values[n * cut : (n + 1) * cut] for n in range(4)]


def once(value, *others):
    return lax.optimization_barrier((value, *others))[0]


def one_hot(rows, source, turned=False):
    place = jnp.arange(rows, dtype=jnp.int32)
    if turned:
        return low(source[:, None] == place[None, :])
    return low(place[:, None] == source[None, :])


def by_distance(size):
    here = {axis: lax.axis_index(axis) for axis in AXES}
    block = size // 128
    place = jnp.arange(size, dtype=jnp.int32)
    r, q = (place % block, place // block)
    c, z, y, x = (q, q // 2, q // 8, q // 32)
    z = (here["z"] + z) % 4
    y = (here["yh"] * 2 + here["yl"] + y) % 4
    x = (here["x"] + x) % 4
    c = (here["c"] + c) % 2
    return ((((y % 2 * 4 + z) * 2 + y // 2) * 4 + x) * 2 + c) * block + r


def by_ring(size, core_first):
    block = size // 128
    place = jnp.arange(size, dtype=jnp.int32)
    r, q = (place % block, place // block)
    if core_first:
        c, x, plane = (q // 64, q // 16, q % 16)
    else:
        c, x, plane = (q, q // 32, q // 2 % 16)
    x = (lax.axis_index("x") + x) % 4
    c = (lax.axis_index("c") + c) % 2
    return ((plane * 4 + x) * 2 + c) * block + r


def body(
    tokens,
    prefix_len,
    query_weight,
    key_weight,
    value_weight,
    mixing_weight,
    gate_weight,
    up_weight,
    down_weight,
    entry_gain,
    mixed_gain,
    middle_gain,
    closing_gain,
    cotangent,
):
    count, width = tokens.shape
    head = key_weight.shape[1]
    heads = query_weight.shape[1] // head
    half = head // 2
    own = gate_weight.shape[0]
    units = down_weight.shape[0]
    units_pad = -(-units // 8) * 8
    hidden_units = 16 * units_pad
    wide = 2 * hidden_units
    own_mix = mixing_weight.shape[0]
    x, c, yh = (lax.axis_index("x"), lax.axis_index("c"), lax.axis_index("yh"))

    def columns(weight):
        cut = weight.reshape(own, 2, 4, 2, 8, units)
        cut = jnp.pad(cut, ((0, 0),) * 5 + ((0, units_pad - units),))
        return cut.transpose(4, 0, 2, 3, 1, 5).reshape(4, 2, own, hidden_units)

    def at(values, index, axis):
        return lax.dynamic_index_in_dim(values, index, axis, keepdims=False)

    mine = heads * head // 2

    def share(core):
        queries = query_weight[:, core * mine : (core + 1) * mine]
        return jnp.concatenate([queries, (key_weight, value_weight)[core]], axis=1)

    def picked(first, second):
        return jnp.where(c == 0, first, second)

    gains_own = jnp.stack([entry_gain, mixed_gain, middle_gain, closing_gain], axis=1)
    gains_own = jnp.pad(gains_own, ((0, 0), (0, 124)))
    kept = jnp.concatenate([picked(share(0), share(1)), gains_own], axis=1)
    given = jnp.concatenate([picked(share(1), share(0)), gains_own], axis=1)
    gate_up = jnp.concatenate([columns(gate_weight), columns(up_weight)], axis=3)
    mixing_own = jnp.pad(mixing_weight, ((0, 0), (0, wide - width)))

    swapped = hop(
        jnp.concatenate([at(gate_up, 1 - c, 1).reshape(4 * own, wide), mixing_own]), "c"
    )
    blocks = hop(given, "c")
    pair_up = jnp.concatenate(
        [at(gate_up, c, 1), swapped[: 4 * own].reshape(4, own, wide)], axis=1
    )
    pair_mixing = jnp.concatenate([mixing_own, swapped[4 * own :]])
    ring = [jnp.concatenate([at(pair_up, (x + n) % 4, 0), pair_mixing]) for n in range(4)]
    blocks = jnp.concatenate([kept, blocks])
    *parts, across = sent(
        *along("x", ring), *((blocks, ("z", n)) for n in (3, 2, 1)), (tokens, "y2")
    )
    ring = jnp.concatenate([ring[0], *parts[:3]])
    blocks = stacked([blocks, *parts[3:]])
    near = jnp.concatenate([tokens, across])
    near, blocks, ring = lax.optimization_barrier((near, blocks, ring))
    back, ahead = sent((near, ("x", 1)), (near, ("x", 3)))
    blocks, back, ahead = lax.optimization_barrier((blocks, back, ahead))
    over, under, *parts = sent(
        (back[:count], ("x", 1)),
        (ahead[count:], ("x", 3)),
        *((blocks, ("y", n)) for n in (3, 2, 1)),
    )
    near = jnp.concatenate([near, back, ahead, over, under])
    blocks = stacked([blocks, *parts])
    far = hop(near, "c")
    chip_rows = jnp.concatenate([tokens, hop(tokens, "c")])
    chunks = [blocks, *(hop(blocks, ("x", n)) for n in (3, 2, 1))]
    def positions(xs, ys, cs):
        place = ((yh ^ ys) * 4 + (x + xs) % 4) * 2 + (c ^ cs)
        return place * count + jnp.arange(count, dtype=jnp.int32)

    query_pos = jnp.concatenate([positions(0, 0, 0), positions(0, 0, 1)])
    key_pos = jnp.concatenate(
        [positions(xs, ys, cs) for cs in (0, 1) for xs in (0, 3, 1, 2) for ys in (0, 1)]
    )
    length = key_pos.shape[0]
    chip = 2 * count
    allowed = (key_pos[None, :] <= query_pos[:, None]) | (key_pos[None, :] < prefix_len[0])
    inverse = 1.0 / THETA ** (jnp.arange(half, dtype=jnp.float32) * (2.0 / head))
    angles = key_pos.astype(jnp.float32)[:, None] * inverse[None, :]
    angles = once(angles, over)
    key_turn = lax.optimization_barrier((jnp.cos(angles), jnp.sin(angles)))
    ring_order = one_hot(width, by_ring(width, False))
    chunks, near_ring, far_ring, chip_ring = lax.optimization_barrier(
        (chunks, *(low(product(rows, ring_order)) for rows in (near, far, chip_rows)))
    )
    turn = tuple(
        jnp.concatenate([t[:count], t[length // 2 : length // 2 + count]]) for t in key_turn
    )

    step = 2 * (own + own_mix)
    place = jnp.arange(4 * step, dtype=jnp.int32)
    q, r = (place // own, place % own)
    up_source = (x - q // 2) % 4 * step + (q % 2 ^ c) * own + r
    q, r = ((place - 8 * own) // own_mix, (place - 8 * own) % own_mix)
    mixing_source = (x - q // 2) % 4 * step + 2 * own + (q % 2 ^ c) * own_mix + r
    source = jnp.where(place < 8 * own, up_source, mixing_source)
    ring = low(outer(one_hot(4 * step, source), ring))
    end = 8 * own
    rest = wide - width
    mixing_half = jnp.where(
        c == 0, ring[end:, :rest], jnp.pad(ring[end:, rest:width], ((0, 0), (0, 2 * rest - width)))
    )
    down_own = jnp.pad(down_weight, ((0, 8 * own_mix - units), (0, 0)))
    plane = lax.all_gather(
        jnp.concatenate([ring[:end], jnp.concatenate([down_own, mixing_half], axis=1)]),
        PLANE,
        axis=0,
    )
    gate_up_full = (
        plane[:, :end].reshape(4, 2, 2, end, wide).transpose(2, 0, 1, 3, 4)
    ).reshape(width, wide)
    mixing_half = plane[:, end:, width:].reshape(-1, rest)
    mixing_other = hop(mixing_half, "c")
    mixing_full = jnp.concatenate(
        [
            jnp.where(c == 0, mixing_half, mixing_other),
            jnp.where(c == 0, mixing_other, mixing_half)[:, : width - rest],
        ],
        axis=1,
    )
    mixing_full = mixing_full.reshape(4, 2, 2, 8 * own_mix, width).transpose(2, 0, 1, 3, 4)
    mixing_full = mixing_full.reshape(heads * head, width)
    down_full = plane[:, end : end + units_pad, :width].reshape(hidden_units, width)

    share_width = mine + head
    order = one_hot(width, by_distance(width))
    share_full = low(product(order, jnp.concatenate([w[:, :share_width] for w in chunks])))
    gains = lax.dot_general(
        jnp.concatenate([w[:, share_width:] for w in chunks]),
        order,
        (((0,), (1,)), ((), ())),
        preferred_element_type=jnp.float32,
    )
    entry_scale, mixed_scale, middle_scale, closing_scale = (gains[k] for k in range(4))

    def turned(pair):
        return (pair[0], -pair[1])


    def scale_of(rows):
        rows = rows.astype(jnp.float32)
        return lax.rsqrt(jnp.mean(rows * rows, axis=-1, keepdims=True) + EPS)

    def normed(rows, scale):
        return low(rows.astype(jnp.float32) * scale * entry_scale)

    near_scale, far_scale, chip_scale = (scale_of(rows) for rows in (near, far, chip_rows))
    pair_raw = jnp.concatenate(
        [
            product(normed(near, near_scale), share_full[:, mine:]),
            product(normed(far, far_scale), share_full[:, mine:]),
        ]
    )
    pair = low(picked(rotate(pair_raw, *key_turn), pair_raw))
    other = hop(pair, "c")
    other = jnp.concatenate([other[length // 2 :], other[: length // 2]])
    all_keys, all_values = (picked(pair, other), picked(other, pair))
    query_raw = product(normed(chip_rows, chip_scale), share_full[:, :mine])
    query_rows = jnp.concatenate(
        [low(rotate(part, *turn) * QSCALE) for part in jnp.split(query_raw, heads // 2, axis=1)]
    )

    bent = jnp.tanh(through(query_rows, all_keys) / CAP)
    expo = jnp.where(
        allowed[None], jnp.exp(CAP * bent - CAP).reshape(heads // 2, chip, length), 0.0
    ).reshape(-1, length)
    probs = expo / jnp.sum(expo, axis=1, keepdims=True)
    mixed_rows = low(product(low(probs), all_values))
    mixed_rows = jnp.concatenate(jnp.split(mixed_rows, heads // 2), axis=1)
    other_heads = hop(mixed_rows[count:], "c")
    attended = picked(
        jnp.concatenate([mixed_rows[:count], other_heads], axis=1),
        jnp.concatenate([other_heads, mixed_rows[:count]], axis=1),
    )
    inputs = tokens.astype(jnp.float32)
    incoming = cotangent.astype(jnp.float32)
    projected = product(attended, mixing_full)
    second = inputs + rms_scale(projected, mixed_scale)
    middle_in = low(rms_scale(second, middle_scale))

    middle_parts = ring_rows(middle_in)
    gates, hiddens = ([], [])
    for rows in middle_parts:
        both = product(rows, gate_up_full)
        gates.append((both[:, :hidden_units], both[:, hidden_units:]))
        hiddens.append(low(gated(*gates[-1])))
    feed = ring_sums(pair_sums(*(low(product(hidden, down_full)) for hidden in hiddens)))
    layer_output = low(second + rms_scale(feed, closing_scale))

    unused, closing_back = jax.vjp(rms_scale, feed, closing_scale)
    feed_grad, closing_term = closing_back(incoming)
    feed_parts = ring_rows(low(feed_grad))
    lows = []
    for rows, pair in zip(feed_parts, gates):
        unused, gated_back = jax.vjp(gated, *pair)
        gate_grad, up_grad = gated_back(through(rows, down_full))
        lows.append(jnp.concatenate([low(gate_grad), low(up_grad)], axis=1))
    both = pair_sums(*(low(through(rows, gate_up_full)) for rows in lows))
    both, *rows_of = lax.optimization_barrier((both, middle_parts, hiddens, feed_parts, lows))
    middle_back = ring_sums(both)
    middle_rows, hidden_rows, feed_rows, low_rows = (jnp.concatenate(parts) for parts in rows_of)
    gate_up_term = low(outer(middle_rows, low_rows))
    down_term = low(outer(hidden_rows, feed_rows))
    gate_up_term = gate_up_term.reshape(2, 4, 2, 8 * own, wide).transpose(1, 2, 0, 3, 4)
    down_term = jnp.pad(
        down_term.reshape(16, units_pad, width), ((0, 0), (0, 0), (0, wide - width))
    )
    plane_term = jnp.concatenate([gate_up_term.reshape(16, 8 * own, wide), down_term], axis=1)
    plane_sum = lax.psum_scatter(
        plane_term.reshape(-1, wide), PLANE, scatter_dimension=0, tiled=True
    )
    down_delta = plane_sum[8 * own : 8 * own + units, :width].astype(jnp.float32)
    tall = 16
    place = jnp.arange(8 * tall, dtype=jnp.int32)
    q, r = (place // tall, place % tall)
    source = ((x + q // 2) % 4 * 2 + (c + q) % 2) * own + r
    source = jnp.where(r < own, source, -1)
    ring = quarters(low(product(one_hot(8 * own, source, True), plane_sum[: 8 * own])))
    ring = [ring[0], *(hop(*pair) for pair in along("x", ring))]
    unused, middle_vjp = jax.vjp(lambda v: rms_scale(v, middle_scale), second)
    second_part = middle_vjp(middle_back)[0]
    second_delta = incoming + second_part
    unused, mixed_vjp = jax.vjp(rms_scale, projected, mixed_scale)
    projected_grad, mixed_term = mixed_vjp(second_delta)
    projected_low = low(projected_grad)
    attended_low = low(through(projected_low, mixing_full))
    mixing_order = one_hot(heads * head, by_ring(heads * head, True))
    attended_near = low(product(attended, mixing_order))
    gain_terms = jnp.pad(jnp.stack([mixed_term, closing_term]), ((0, 6), (0, 0)))
    gain_terms = low(product(low(gain_terms), ring_order))
    back_kept = picked(attended_low[:, :mine], attended_low[:, mine:])
    back_given = picked(attended_low[:, mine:], attended_low[:, :mine])
    mixing_given = low(outer(attended_near[:, mine:], projected_low))
    back_got, mixing_got = (hop(back_given, "c"), hop(mixing_given, "c"))
    mixing_term = low(
        outer(attended_near[:, :mine], projected_low) + mixing_got.astype(jnp.float32)
    )
    back_rows = jnp.concatenate([back_kept, back_got])
    back_rows = jnp.concatenate(jnp.split(back_rows, heads // 2, axis=1))
    prob_back = through(back_rows, all_values)
    weighted = jnp.sum(prob_back * probs, axis=1, keepdims=True)
    capped_back = probs * (prob_back - weighted)
    score_low = low(capped_back * (1.0 - bent * bent))
    query_back = product(score_low, all_keys)
    query_grad = jnp.concatenate(
        [
            rotate(part * QSCALE, *turned(turn))
            for part in jnp.split(query_back, heads // 2)
        ],
        axis=1,
    )
    query_low = low(query_grad)

    query_terms = quarters(low(outer(chip_ring, low(query_grad * chip_scale))))
    query_terms, score_low, probs_low, back_rows = lax.optimization_barrier(
        (query_terms, score_low, low(probs), back_rows)
    )
    value_term = outer(probs_low, back_rows)
    key_term = outer(score_low, query_rows)
    given = low(picked(value_term, key_term))
    given = jnp.concatenate([given[length // 2 :], given[: length // 2]])
    cut = width // 4
    query_parts = [hop(*pair) for pair in along("x", query_terms)]
    pair_got = hop(given, "c")
    with_gains = [
        jnp.concatenate(
            [part, jnp.pad(gain_terms[:, n * cut : (n + 1) * cut], ((0, 0), (0, width - cut)))]
        )
        for n, part in enumerate(quarters(mixing_term))
    ]
    mixing_parts = [hop(*pair) for pair in along("x", with_gains)]
    pair_term = picked(key_term, value_term) + pair_got.astype(jnp.float32)
    pair_low = picked(rotate(pair_term, *turned(key_turn)), pair_term)
    pair_terms = quarters(
        low(
            outer(near_ring, low(pair_low[: length // 2] * near_scale))
            + outer(far_ring, low(pair_low[length // 2 :] * far_scale))
        )
    )
    pair_terms, query_parts = lax.optimization_barrier((pair_terms, query_parts))
    pair_parts = [hop(*pair) for pair in along("x", pair_terms)]
    pair_cut, pair_parts, mixing_parts = lax.optimization_barrier(
        (low(pair_term), pair_parts, mixing_parts)
    )
    pair_cut = pair_cut.reshape(2, 4, -1, head)
    sums = [pair_cut[:, k].reshape(-1, head) for k in range(4)]
    back, ahead, beyond = (hop(sums[1], ("x", 3)), hop(sums[2], ("x", 1)), hop(sums[3], ("x", 2)))
    pair_sum = added(sums[0], (back, ahead, beyond)).reshape(2, 2, count, head)
    query_sum = added(query_terms[0], query_parts)
    mixing_sum = added(with_gains[0], mixing_parts)
    gain_columns = outer(mixing_sum[-8:, :cut], jnp.eye(8, 128, dtype=jnp.float32))
    share_sum = low(
        jnp.concatenate([query_sum, added(pair_terms[0], pair_parts), gain_columns], axis=1)
    )
    pair_own = 2 * own
    place = jnp.arange(16 * 24, dtype=jnp.int32)
    source = jnp.where(place % 24 < pair_own, place // 24 * pair_own + place % 24, -1)
    share_blocks = low(product(one_hot(cut, source, True), share_sum)).reshape(16, 24, -1)
    span = share_blocks.shape[2]
    mixing_blocks = low(mixing_sum[:-8]).reshape(16, own_mix, width)
    slack = ((0, 0), (0, 0), (0, 2 * span - width))
    plane_blocks = jnp.concatenate(
        [share_blocks, mixing_blocks[..., :span], jnp.pad(mixing_blocks[..., span:], slack)],
        axis=1,
    )
    block = plane_blocks.shape[1]
    plane_parts = lax.all_to_all(
        plane_blocks.reshape(-1, span), ("yl", "z", "yh"), 0, 0, tiled=True
    )
    ring[0], pair_sum = lax.optimization_barrier((ring[0], pair_sum))
    ring = stacked(ring)
    ring_got = hop(ring, "c")
    place = jnp.arange(8 * own, dtype=jnp.int32)
    q, r = (place // own, place % own)
    source = (x - q // 2) % 4 * 2 * tall + r
    other = (c + q) % 2 == 1
    gate_up_sum = product(
        one_hot(8 * tall, jnp.where(other, -1, source), True), ring
    ) + product(one_hot(8 * tall, jnp.where(other, source + tall, -1), True), ring_got)
    gate_up_sum = low(gate_up_sum).reshape(8, own, 2, 4, 2, 2, units_pad)
    gate_up_sum = gate_up_sum[..., :units].transpose(2, 1, 5, 3, 4, 0, 6).reshape(2, own, -1)
    pair_got = hop(low(pair_sum[:, 1]), "y2")
    pair_sum = (pair_sum[:, 0] + pair_got.astype(jnp.float32)).reshape(chip, head)
    pair_low = low(picked(rotate(pair_sum, *turned(turn)), pair_sum))
    chip_back = through(jnp.concatenate([query_low, pair_low], axis=1), share_full)
    back_got = hop(low(chip_back[count:]), "c")
    plane_parts, gate_up_sum, back_got = lax.optimization_barrier(
        (plane_parts, gate_up_sum, back_got)
    )
    plane_total = jnp.sum(plane_parts.reshape(16, block, span).astype(jnp.float32), axis=0)
    share_sum = plane_total[:pair_own]
    mixing_delta = jnp.concatenate(
        [plane_total[24 : 24 + own_mix], plane_total[24 + own_mix :, : width - span]], axis=1
    )
    share_kept, share_got = (share_sum[:own], hop(low(share_sum[own:]), "c").astype(jnp.float32))
    first = picked(share_kept, share_got)
    second_share = picked(share_got, share_kept)
    share_delta = jnp.concatenate(
        [
            first[:, :mine],
            second_share[:, :mine],
            first[:, mine:share_width],
            second_share[:, mine:share_width],
        ],
        axis=1,
    )
    entry_delta = jnp.sum(
        jnp.concatenate([query_weight, key_weight, value_weight], axis=1) * share_delta, axis=1
    )
    share_delta = share_delta * entry_gain.astype(jnp.float32)[:, None]
    query_delta, key_delta, value_delta = jnp.split(
        share_delta, [2 * mine, 2 * mine + head], axis=1
    )
    gain_deltas = (first + second_share)[:, share_width:]
    mixed_delta, closing_delta = (gain_deltas[:, 0], gain_deltas[:, 1])
    entry_back = chip_back[:count] + back_got.astype(jnp.float32)
    unused, entry_vjp = jax.vjp(lambda v: rms_scale(v, entry_scale), inputs)
    input_delta = second_delta + entry_vjp(entry_back)[0]

    gate_delta, up_delta = (part.astype(jnp.float32) for part in gate_up_sum)

    middle_delta = jnp.sum(
        gate_weight.astype(jnp.float32) * gate_delta + up_weight.astype(jnp.float32) * up_delta,
        axis=1,
    ) / middle_gain.astype(jnp.float32)
    return (
        layer_output,
        input_delta,
        query_delta,
        key_delta,
        value_delta,
        mixing_delta,
        gate_delta,
        up_delta,
        down_delta,
        entry_delta,
        mixed_delta,
        middle_delta,
        closing_delta,
    )


def solution(mesh):
    cut = Mesh(mesh.devices.reshape(SIZES), AXES)
    rows = P(AXES, None)
    flat = P(AXES)
    in_specs = (rows, P(("yl", "z")), *(rows,) * 7, *(flat,) * 4, rows)
    out_specs = (*(rows,) * 9, *(flat,) * 4)
    return jax.shard_map(body, mesh=cut, in_specs=in_specs, out_specs=out_specs, check_vma=False)
```
